512 devices in a mesh: dp: 16 (over x, y), expert: 32 (over z, core).
Axes of the slice: x: 4, y: 4, z: 16, core: 2. Of those that a mesh axis runs over, the one named last changes fastest.
Arguments:
- upstream: bfloat16 [65536, 2048], P(('dp', 'expert')), may hold values from -6 to 6
- expert_ids: int32 [65536, 8], P(('dp', 'expert')), may hold values from 0 to 63, all different within a row; in each aligned block of 128 rows (0 to 127, 128 to 255, ...) at most 18 rows name the same one
- route_probs: bfloat16 [65536, 8], P(('dp', 'expert')), may hold values from 0.029907227 to 0.29882812
- saved_hidden: bfloat16 [16, 64, 32, 18, 768], P('dp', 'expert'), may hold values from -1 to 1
- down_weight: bfloat16 [64, 768, 2048], P('expert', 'dp'), may hold values from -0.21875 to 0.21875
- trained: int32 [64], P('expert'), may hold values from 0 to 1, as said below
Outputs:
- hidden_grad: bfloat16 [16, 64, 32, 18, 768], P('dp', 'expert')
- prob_grad: float32 [65536, 8], P(('dp', 'expert'))
- down_grad: float32 [32, 768, 2048], P('expert', 'dp')
The draws below stay inside these ranges and needn't reach their ends.
Inputs may be any that keep to these rules, and one draw needn't show every extreme that they name: `expert_ids`: among the 128 tokens of one device no expert is chosen more than 18 times, a bound that some block reaches; a token chooses 8 different experts. `trained`: among experts j * 2 to (j + 1) * 2 - 1 at most one is 1, and among the first 2 exactly one.
All inputs are finite; a program needn't handle non-finite values.
Results may differ from the reference program's by a relative error of at most 0.015.
Values may be sent and summed in bfloat16 or wider, within the bound.
No kernel may reach another device: no remote copies, remote signals or barrier semaphores. Data moves between devices by JAX's collectives and lax.ppermute only.
A program may use at most 128 MiB of HBM per device.

```python
import math
import jax
import jax.numpy as jnp
import numpy as np
from jax import lax

D = 2048
H = 768
EXP_DEV = 2
TOP = 8
TOK_DEV = 128
EXPERTS = 64
CAP = 18
TOKENS = 65536
N_DP = 16
N_EXPERT = 32
DEVICES = 512


def draw_trained(key, part):
    key = jax.random.fold_in(key, 3)
    groups = EXPERTS // EXP_DEV
    first_key, second_key = jax.random.split(key)
    present = jax.random.randint(first_key, (groups,), 0, 4) > 0
    present = present.at[0].set(True)
    which_one = jax.random.randint(second_key, (groups,), 0, EXP_DEV)
    local_ids = jnp.arange(EXP_DEV, dtype=jnp.int32)
    chosen = present[:, None] & (local_ids[None, :] == which_one[:, None])
    return chosen.astype(jnp.int32).reshape(EXPERTS)


def steps_of(stream_key, dims, cuts, smallest, high):
    loudness = 1.0
    for dim, parts in cuts:
        draws = jax.random.uniform(jax.random.fold_in(jax.random.fold_in(stream_key, 6), dim), (parts,), jnp.float32, smallest / len(cuts), high / len(cuts))
        loudness = loudness * jnp.repeat(jnp.exp(draws), dims[dim] // parts).reshape((-1,) + (1,) * (len(dims) - 1 - dim))
    return loudness


def shared_out(rng, own, number, rows, amount, top, bound, lean):
    order = jax.random.permutation(rng, amount)
    packed, common = portions_of(amount, rows * top, bound, lean, True), portions_of(amount, rows * top, bound, lean, False)
    places = jnp.arange(amount)

    def named(sizes, rotation):
        used = int((sizes > 0).sum())
        fixed = max(1, used // 4)
        passed = fixed + (places - fixed + rotation * (used - fixed)) % max(1, amount - fixed)
        return jnp.zeros((amount,), jnp.int32).at[order[jnp.where(places < fixed, places, passed)]].set(jnp.asarray(sizes, jnp.int32))

    sizes = jnp.where(number % 4 == 0, named(packed, number // 4), named(common, number - number // 4 - 1))
    mixed = jax.random.permutation(jax.random.fold_in(own, 3), amount)
    donor, receiver = mixed[0:amount // 2 * 2:2], mixed[1:amount // 2 * 2:2]
    margin = jnp.minimum(sizes[donor] - 1, bound - sizes[receiver]) // 2
    margin = jnp.where((donor == order[0]) | (receiver == order[0]) | (sizes[receiver] == 0), 0, jnp.maximum(margin, 0))
    passed = jax.random.randint(jax.random.fold_in(own, 4), (amount // 2,), 0, 1 << 20) % (margin + 1)
    sizes = sizes.at[donor].add(-passed).at[receiver].add(passed)
    labels = jnp.searchsorted(jnp.cumsum(sizes), jnp.arange(rows * top), side="right").astype(jnp.int32)
    grid = labels.reshape(top, rows).T
    grid = grid[jax.random.permutation(jax.random.fold_in(own, 1), rows)]
    rotation = jax.random.randint(jax.random.fold_in(own, 2), (rows, 1), 0, top)
    return jnp.take_along_axis(grid, (jnp.arange(top)[None, :] + rotation) % top, axis=1)


def portions_of(number_of, total, limit, skew, full):
    portions = [(1 << 20) // math.isqrt(rank ** skew) + 1 for rank in range(1, number_of + 1)]
    largest = limit if full else min(limit, max(-(-total // number_of), total * portions[0] // sum(portions)))
    least = 1 if total - largest >= number_of - 1 else 0
    given, spare = [largest] + [least] * (number_of - 1), total - largest - least * (number_of - 1)
    while spare > 0:
        free = [i for i in range(1, number_of) if given[i] < largest] or [i for i in range(1, number_of) if given[i] < limit]
        whole, remaining = sum([portions[i] for i in free]), spare
        for i in free:
            extra = min(limit - given[i], max(1, remaining * portions[i] // whole), spare)
            given[i] = given[i] + extra
            spare = spare - extra
    return np.array(given)


def normal_values(rng, shape, width, reach, cuts=(), kind=jnp.bfloat16):
    gain = steps_of(rng, shape, cuts, -0.22, 0.18) if cuts else 1.0
    result = jax.random.normal(rng, shape, jnp.float32) * width * gain
    return jnp.minimum(jnp.maximum(result, -reach), reach).astype(kind)


def setup_inputs(seed: int = 0) -> dict:
    splits = jax.random.split(jax.random.key(seed), 7)
    upstream = normal_values(splits[0], (TOKENS, D), 1.0, 6.0, ((0, 512),))
    expert_ids_keys = jax.random.split(jax.random.fold_in(splits[1], 1), TOKENS // TOK_DEV)
    expert_ids_turns = jax.random.permutation(jax.random.fold_in(splits[1], 3), TOKENS // TOK_DEV)
    expert_ids = jax.vmap(lambda own, number: shared_out(jax.random.fold_in(splits[1], 2), own, number, TOK_DEV, EXPERTS, TOP, CAP, 2))(expert_ids_keys, expert_ids_turns).reshape((TOKENS, TOP))
    route_probs = jnp.clip(jnp.exp(math.log(0.29882812) - 2.30176843 * jax.random.uniform(splits[2], (TOKENS, TOP), jnp.float32) ** steps_of(splits[2], (TOKENS, TOP), ((0, 512),), -0.2, 0.2)), 0.029907227, 0.29882812).astype(jnp.bfloat16)
    saved_hidden = normal_values(splits[3], (N_DP, EXPERTS, N_EXPERT, CAP, H), 0.15, 1.0, ((0, 16), (1, 32)))
    down_weight = normal_values(splits[4], (EXPERTS, H, D), H ** -0.5, 0.21875, ((0, 32), (1, 16)))
    trained = draw_trained(jax.random.fold_in(splits[6], 71), 0)
    return {"upstream": upstream, "expert_ids": expert_ids, "route_probs": route_probs, "saved_hidden": saved_hidden, "down_weight": down_weight, "trained": trained}


def slot_table(expert_ids):
    flat_ids = expert_ids.reshape(DEVICES, TOK_DEV * TOP)
    choices_all = jnp.arange(EXPERTS, dtype=jnp.int32)
    onehot = (flat_ids[:, :, None] == choices_all[None, None, :]).astype(jnp.int32)
    rank_table = jnp.cumsum(onehot, axis=1) - 1
    slot_of = jnp.take_along_axis(rank_table, flat_ids[:, :, None], axis=2)[:, :, 0]
    return slot_of.reshape(TOKENS, TOP).astype(jnp.int32)

def reference(upstream, expert_ids, route_probs, saved_hidden, down_weight, trained):
    slot_of = slot_table(expert_ids)
    token_ids = jnp.arange(TOKENS, dtype=jnp.int32)
    device_of = token_ids // TOK_DEV
    replica = jnp.broadcast_to((device_of // N_EXPERT)[:, None], (TOKENS, TOP))
    source = jnp.broadcast_to((device_of % N_EXPERT)[:, None], (TOKENS, TOP))
    token_tab = jnp.broadcast_to(token_ids[:, None], (TOKENS, TOP))
    shape_tab = (N_DP, EXPERTS, N_EXPERT, CAP)
    row_table = jnp.zeros(shape_tab, jnp.int32).at[replica, expert_ids, source, slot_of].set(token_tab)
    prob_table = jnp.zeros(shape_tab, jnp.float32).at[replica, expert_ids, source, slot_of].set(route_probs.astype(jnp.float32))

    def one_group(group_id):
        hidden_parts = []
        score_parts = []
        grad_total = jnp.zeros((H, D), jnp.float32)
        for local_id in range(EXP_DEV):
            expert_id = group_id * EXP_DEV + local_id
            gather_rows = lax.dynamic_index_in_dim(row_table, expert_id, 1, keepdims=False)
            weighting = lax.dynamic_index_in_dim(prob_table, expert_id, 1, keepdims=False)[..., None]
            rows_in = upstream[gather_rows].astype(jnp.float32)
            weight_one = lax.dynamic_index_in_dim(down_weight, expert_id, 0, keepdims=False).astype(jnp.float32)
            saved_one = lax.dynamic_index_in_dim(saved_hidden, expert_id, 1, keepdims=False).astype(jnp.float32)
            grad_slots = jnp.einsum('rscd,hd->rsch', rows_in, weight_one)
            hidden_parts.append((weighting * grad_slots).astype(jnp.bfloat16))
            score_parts.append(lax.optimization_barrier(jnp.sum(grad_slots * saved_one, axis=3)))
            scaled_rows = (weighting * rows_in).astype(jnp.bfloat16).astype(jnp.float32)
            is_trained = lax.dynamic_index_in_dim(trained, expert_id, 0, keepdims=False)

            def compute_grad():
                partial_sums = jnp.einsum('rsch,rscd->rhd', saved_one, scaled_rows)
                rounded = lax.optimization_barrier(partial_sums.astype(jnp.bfloat16))
                return lax.optimization_barrier(jnp.sum(rounded.astype(jnp.float32), axis=0))

            def no_grad():
                return jnp.zeros((H, D), jnp.float32)
            grad_total = grad_total + lax.cond(is_trained > 0, compute_grad, no_grad)
        return (jnp.stack(hidden_parts), jnp.stack(score_parts), grad_total)
    hidden_all, score_all, down_grad = lax.map(one_group, jnp.arange(N_EXPERT, dtype=jnp.int32))
    hidden_grad = jnp.transpose(hidden_all, (2, 0, 1, 3, 4, 5)).reshape(N_DP, EXPERTS, N_EXPERT, CAP, H)
    slot_scores = jnp.transpose(score_all, (2, 0, 1, 3, 4)).reshape(N_DP, EXPERTS, N_EXPERT, CAP)
    prob_grad = slot_scores[replica, expert_ids, source, slot_of]
    return (hidden_grad, prob_grad, down_grad)
```

```python
import functools

import jax
import jax.numpy as jnp
from jax import lax
from jax.experimental import pallas as pl
from jax.experimental.pallas import tpu as pltpu
from jax.sharding import PartitionSpec as P

GROUP = 8


def pack_kernel(flags, tokens, token_of, weights, saved_t, rows, term, scaled):
    step = pl.program_id(0)
    width = tokens.shape[0]
    group_rows = token_of.shape[1]
    first = jnp.maximum(flags[0], flags[1]) > 0
    second = flags[1] > 0
    packed = []
    for j in range(token_of.shape[0]):
        lanes = lax.broadcasted_iota(jnp.int32, (group_rows, width), 1)
        choose = (lanes == token_of[j]).astype(jnp.bfloat16)
        block = jnp.dot(choose, tokens[...], preferred_element_type=jnp.float32)
        rows[j] = block.astype(jnp.bfloat16)
        packed.append(weights[j] * block)
    chosen = jnp.where(second, packed[1], packed[0])
    chosen = jnp.where(first, chosen, 0.0).astype(jnp.bfloat16)
    scaled[pl.ds(pl.multiple_of(step * group_rows, 16), group_rows), :] = chosen

    @pl.when(step == pl.num_programs(0) - 1)
    def _():
        span = 512
        for n in range(term.shape[1] // span):
            cut = slice(n * span, (n + 1) * span)
            term[:, cut] = jnp.dot(
                saved_t[...], scaled[:, cut], preferred_element_type=jnp.float32
            ).astype(jnp.bfloat16)


def grad_kernel(rows, weight, saved, probs, hidden, scores):
    grads = lax.dot_general(
        rows[0],
        weight[:, 0].reshape(-1, weight.shape[-1]),
        (((1,), (1,)), ((), ())),
        preferred_element_type=jnp.float32,
    )
    hidden[0] = (probs[0] * grads).astype(jnp.bfloat16)
    scores[0] = jnp.sum(grads * saved[0].astype(jnp.float32), axis=1, keepdims=True)


def pack(tokens, token_of, weights, saved_t, flags):
    count, model = tokens.shape
    experts, slots, _ = token_of.shape
    hidden = saved_t.shape[0]
    steps = count // (GROUP * 128)
    part = slots // steps
    return pl.pallas_call(
        pack_kernel,
        grid=(steps,),
        in_specs=[
            pl.BlockSpec(memory_space=pltpu.SMEM),
            pl.BlockSpec((GROUP * 128, model), lambda i: (i, 0)),
            pl.BlockSpec((experts, part, 1), lambda i: (0, i, 0)),
            pl.BlockSpec((experts, part, 1), lambda i: (0, i, 0)),
            pl.BlockSpec((hidden, slots), lambda i: (0, 0)),
        ],
        out_specs=[
            pl.BlockSpec((experts, part, model), lambda i: (0, i, 0)),
            pl.BlockSpec((hidden, model), lambda i: (0, 0)),
        ],
        out_shape=[
            jax.ShapeDtypeStruct((experts, slots, model), jnp.bfloat16),
            jax.ShapeDtypeStruct((hidden, model), jnp.bfloat16),
        ],
        scratch_shapes=[pltpu.VMEM((slots, model), jnp.bfloat16)],
        compiler_params=pltpu.CompilerParams(vmem_limit_bytes=48 << 20),
        cost_estimate=pl.CostEstimate(
            flops=2 * experts * slots * GROUP * 128 * model + 2 * hidden * slots * model,
            bytes_accessed=2 * (count + experts * slots + hidden) * model,
            transcendentals=0,
        ),
    )(flags, tokens, token_of, weights, saved_t)


def grads_of(rows, weight, saved, probs):
    experts, slots, model = rows.shape
    hidden = saved.shape[-1]
    halves = 2
    part = slots // halves
    shards, _, shard, _ = weight.shape
    return pl.pallas_call(
        grad_kernel,
        grid=(experts, halves),
        in_specs=[
            pl.BlockSpec((1, part, model), lambda j, i: (j, i, 0)),
            pl.BlockSpec((shards, 1, shard, model), lambda j, i: (0, j, 0, 0)),
            pl.BlockSpec((1, part, hidden), lambda j, i: (j, i, 0)),
            pl.BlockSpec((1, part, 1), lambda j, i: (j, i, 0)),
        ],
        out_specs=[
            pl.BlockSpec((1, part, hidden), lambda j, i: (j, i, 0)),
            pl.BlockSpec((1, part, 1), lambda j, i: (j, i, 0)),
        ],
        out_shape=[
            jax.ShapeDtypeStruct((experts, slots, hidden), jnp.bfloat16),
            jax.ShapeDtypeStruct((experts, slots, 1), jnp.float32),
        ],
        compiler_params=pltpu.CompilerParams(vmem_limit_bytes=48 << 20),
        cost_estimate=pl.CostEstimate(
            flops=2 * experts * slots * hidden * model,
            bytes_accessed=2 * experts * (slots + hidden) * model + 4 * experts * slots * hidden,
            transcendentals=0,
        ),
    )(rows, weight, saved, probs)


def on_device(upstream, expert_ids, route_probs, saved_hidden, down_weight, trained):
    tok_rows, model = upstream.shape
    top = expert_ids.shape[1]
    groups = lax.axis_size("expert")
    replicas = lax.axis_size("dp")
    exp_dev, shard, _ = down_weight.shape
    capacity, hidden = saved_hidden.shape[3:]
    slots = groups * capacity

    tokens = lax.all_gather(upstream, "expert", axis=0, tiled=True)

    weight = lax.all_to_all(
        jnp.broadcast_to(down_weight[None], (replicas, exp_dev, shard, model)),
        "dp", split_axis=0, concat_axis=0, tiled=True,
    )

    routing = jnp.concatenate([expert_ids.T.astype(jnp.bfloat16), route_probs.T], axis=0)
    routing = lax.all_gather(routing, "expert", axis=0, tiled=True)
    routing = routing.reshape(groups, 2 * top, tok_rows)
    ids = routing[:, :top].astype(jnp.int32)
    probs = routing[:, top:].astype(jnp.float32)
    own = lax.axis_index("expert") * exp_dev + jnp.arange(exp_dev, dtype=jnp.int32)
    named = ids[None] == own[:, None, None, None]
    taken = jnp.any(named, axis=2)
    prob_of = jnp.sum(jnp.where(named, probs[None], 0.0), axis=2)
    place = jnp.arange(tok_rows, dtype=jnp.int32)
    earlier = (place[:, None] < place[None, :]).astype(jnp.bfloat16)
    rank = lax.dot_general(
        taken.astype(jnp.bfloat16), earlier, (((2,), (0,)), ((), ())),
        preferred_element_type=jnp.float32,
    ).astype(jnp.int32)
    at_slot = taken[:, :, None, :] & (
        rank[:, :, None, :] == jnp.arange(capacity, dtype=jnp.int32)[None, None, :, None]
    )
    local = (jnp.arange(groups, dtype=jnp.int32) % GROUP)[:, None] * tok_rows + place[None, :]
    token_of = jnp.max(jnp.where(at_slot, local[None, :, None, :], -1), axis=3)
    slot_prob = jnp.sum(jnp.where(at_slot, prob_of[:, :, None, :], 0.0), axis=3)
    token_of = token_of.reshape(exp_dev, slots, 1)
    slot_prob = slot_prob.reshape(exp_dev, slots, 1)

    saved = saved_hidden[0].reshape(exp_dev, slots, hidden)
    saved_t = jnp.where(trained[1] > 0, saved[1], saved[0]).T

    rows, term = pack(tokens, token_of, slot_prob, saved_t, trained)
    terms = lax.all_to_all(
        term.reshape(replicas, shard, model), "dp", split_axis=0, concat_axis=0, tiled=True
    )
    hidden_grad, scores = grads_of(rows, weight, saved, slot_prob)
    scores = scores.reshape(exp_dev, groups, capacity)
    by_token = jnp.sum(jnp.where(at_slot, scores[..., None], 0.0), axis=2)
    by_token = by_token.transpose(1, 0, 2).reshape(groups, 1, exp_dev * tok_rows)
    returned = lax.all_to_all(by_token, "expert", split_axis=0, concat_axis=0, tiled=True)
    returned = returned.reshape(groups * exp_dev, tok_rows)
    every = jnp.arange(groups * exp_dev, dtype=jnp.int32)
    chose = expert_ids.T[:, None, :] == every[None, :, None]
    prob_grad = jnp.sum(jnp.where(chose, returned[None], 0.0), axis=1).T
    down_grad = jnp.sum(terms.astype(jnp.float32), axis=0)
    hidden_grad = hidden_grad.reshape(1, exp_dev, groups, capacity, hidden)
    return hidden_grad, prob_grad, down_grad[None]


def solution(mesh):
    tokens = P(("dp", "expert"), None)
    slots = P("dp", "expert", None, None, None)
    weights = P("expert", "dp", None)
    return jax.shard_map(
        on_device,
        mesh=mesh,
        in_specs=(tokens, tokens, tokens, slots, weights, P("expert")),
        out_specs=(slots, tokens, weights),
        check_vma=False,
    )
```

```python
import functools

import jax
import jax.numpy as jnp
from jax import lax
from jax.experimental import pallas as pl
from jax.experimental.pallas import tpu as pltpu
from jax.sharding import PartitionSpec as P

GROUP = 8
PAIRS = 4


def pack_kernel(flags, tokens, token_of, weights, saved_t, rows, term, scaled):
    step = pl.program_id(0)
    part = PAIRS * 128
    experts, group_rows, _ = token_of.shape
    packs = group_rows * PAIRS // GROUP
    first = jnp.maximum(flags[0], flags[1]) > 0
    second = flags[1] > 0
    lanes = lax.broadcasted_iota(jnp.int32, (experts * packs, part), 1)
    choices = []
    for h in range(GROUP // PAIRS):
        wanted = jnp.concatenate(
            [token_of[j, h * packs:(h + 1) * packs] for j in range(experts)], axis=0
        )
        choices.append((lanes == wanted).astype(jnp.bfloat16))
    span = 512
    for n in range(tokens.shape[1] // span):
        cut = slice(n * span, (n + 1) * span)
        blocks = [
            jnp.dot(choose, tokens[h * part:(h + 1) * part, cut], preferred_element_type=jnp.float32)
            for h, choose in enumerate(choices)
        ]
        packed = []
        for j in range(experts):
            block = jnp.concatenate([b[j * packs:(j + 1) * packs] for b in blocks], axis=0)
            rows[j, :, cut] = block.astype(jnp.bfloat16)
            packed.append(weights[j] * block)
        chosen = jnp.where(second, packed[1], packed[0])
        chosen = jnp.where(first, chosen, 0.0).astype(jnp.bfloat16)
        scaled[pl.ds(pl.multiple_of(step * group_rows, 16), group_rows), cut] = chosen

    @pl.when(step == pl.num_programs(0) - 1)
    def _():
        for n in range(term.shape[1] // span):
            cut = slice(n * span, (n + 1) * span)
            term[:, cut] = jnp.dot(
                saved_t[...], scaled[:, cut], preferred_element_type=jnp.float32
            ).astype(jnp.bfloat16)


def grad_kernel(rows, weight, saved, probs, hidden, scores):
    grads = lax.dot_general(
        rows[0],
        weight[:, 0].reshape(-1, weight.shape[-1]),
        (((1,), (1,)), ((), ())),
        preferred_element_type=jnp.float32,
    )
    hidden[0] = (probs[0] * grads).astype(jnp.bfloat16)
    scores[0] = jnp.sum(grads * saved[0].astype(jnp.float32), axis=1, keepdims=True)


def pack(tokens, token_of, weights, saved_t, flags):
    count, model = tokens.shape
    experts, slots, _ = token_of.shape
    hidden = saved_t.shape[0]
    steps = count // (GROUP * 128)
    part = slots // steps
    return pl.pallas_call(
        pack_kernel,
        grid=(steps,),
        in_specs=[
            pl.BlockSpec(memory_space=pltpu.SMEM),
            pl.BlockSpec((GROUP * 128, model), lambda i: (i, 0)),
            pl.BlockSpec((experts, part, 1), lambda i: (0, i, 0)),
            pl.BlockSpec((experts, part, 1), lambda i: (0, i, 0)),
            pl.BlockSpec((hidden, slots), lambda i: (0, 0)),
        ],
        out_specs=[
            pl.BlockSpec((experts, part, model), lambda i: (0, i, 0)),
            pl.BlockSpec((hidden, model), lambda i: (0, 0)),
        ],
        out_shape=[
            jax.ShapeDtypeStruct((experts, slots, model), jnp.bfloat16),
            jax.ShapeDtypeStruct((hidden, model), jnp.bfloat16),
        ],
        scratch_shapes=[pltpu.VMEM((slots, model), jnp.bfloat16)],
        compiler_params=pltpu.CompilerParams(vmem_limit_bytes=48 << 20),
        cost_estimate=pl.CostEstimate(
            flops=2 * experts * slots * PAIRS * 128 * model + 2 * hidden * slots * model,
            bytes_accessed=2 * (count + experts * slots + hidden) * model,
            transcendentals=0,
        ),
    )(flags, tokens, token_of, weights, saved_t)


def grads_of(rows, weight, saved, probs):
    experts, slots, model = rows.shape
    hidden = saved.shape[-1]
    halves = 2
    part = slots // halves
    shards, _, shard, _ = weight.shape
    return pl.pallas_call(
        grad_kernel,
        grid=(experts, halves),
        in_specs=[
            pl.BlockSpec((1, part, model), lambda j, i: (j, i, 0)),
            pl.BlockSpec((shards, 1, shard, model), lambda j, i: (0, j, 0, 0)),
            pl.BlockSpec((1, part, hidden), lambda j, i: (j, i, 0)),
            pl.BlockSpec((1, part, 1), lambda j, i: (j, i, 0)),
        ],
        out_specs=[
            pl.BlockSpec((1, part, hidden), lambda j, i: (j, i, 0)),
            pl.BlockSpec((1, part, 1), lambda j, i: (j, i, 0)),
        ],
        out_shape=[
            jax.ShapeDtypeStruct((experts, slots, hidden), jnp.bfloat16),
            jax.ShapeDtypeStruct((experts, slots, 1), jnp.float32),
        ],
        compiler_params=pltpu.CompilerParams(vmem_limit_bytes=48 << 20),
        cost_estimate=pl.CostEstimate(
            flops=2 * experts * slots * hidden * model,
            bytes_accessed=2 * experts * (slots + hidden) * model + 4 * experts * slots * hidden,
            transcendentals=0,
        ),
    )(rows, weight, saved, probs)


def slot_tables(ids, experts, capacity):
    named = ids[None] == experts[:, None, None, None]
    taken = jnp.any(named, axis=2)
    place = jnp.arange(ids.shape[-1], dtype=jnp.int32)
    earlier = (place[:, None] < place[None, :]).astype(jnp.bfloat16)
    rank = lax.dot_general(
        taken.astype(jnp.bfloat16), earlier, (((2,), (0,)), ((), ())),
        preferred_element_type=jnp.float32,
    ).astype(jnp.int32)
    each = jnp.arange(capacity, dtype=jnp.int32)[None, None, :, None]
    return named, taken, taken[:, :, None, :] & (rank[:, :, None, :] == each)


def on_device(upstream, expert_ids, route_probs, saved_hidden, down_weight, trained):
    tok_rows, model = upstream.shape
    top = expert_ids.shape[1]
    groups = lax.axis_size("expert")
    replicas = lax.axis_size("dp")
    exp_dev, shard, _ = down_weight.shape
    capacity, hidden = saved_hidden.shape[3:]
    slots = groups * capacity

    tokens = lax.all_gather(upstream, "expert", axis=0, tiled=True)

    weight = lax.all_to_all(
        jnp.broadcast_to(down_weight[None], (replicas, exp_dev, shard, model)),
        "dp", split_axis=0, concat_axis=0, tiled=True,
    )

    routing = jnp.concatenate([expert_ids.T.astype(jnp.bfloat16), route_probs.T], axis=0)
    routing = lax.all_gather(routing, "expert", axis=0, tiled=True)
    routing = routing.reshape(groups, 2 * top, tok_rows)
    ids = routing[:, :top].astype(jnp.int32)
    probs = routing[:, top:].astype(jnp.float32)
    me = lax.axis_index("expert")
    own = me * exp_dev + jnp.arange(exp_dev, dtype=jnp.int32)
    named, taken, at_slot = slot_tables(ids, own, capacity)
    prob_of = jnp.sum(jnp.where(named, probs[None], 0.0), axis=2)
    place = jnp.arange(tok_rows, dtype=jnp.int32)
    local = (jnp.arange(groups, dtype=jnp.int32) % PAIRS)[:, None] * tok_rows + place[None, :]
    token_of = jnp.max(jnp.where(at_slot, local[None, :, None, :], -1), axis=3)
    slot_prob = jnp.sum(jnp.where(at_slot, prob_of[:, :, None, :], 0.0), axis=3)
    token_of = token_of.reshape(exp_dev, slots, 1)
    slot_prob = slot_prob.reshape(exp_dev, slots, 1)

    saved = saved_hidden[0].reshape(exp_dev, slots, hidden)
    saved_t = jnp.where(trained[1] > 0, saved[1], saved[0]).T

    rows, term = pack(tokens, token_of, slot_prob, saved_t, trained)
    terms = lax.all_to_all(
        term.reshape(replicas, shard, model), "dp", split_axis=0, concat_axis=0, tiled=True
    )
    hidden_grad, scores = grads_of(rows, weight, saved, slot_prob)
    scores = lax.all_gather(scores.reshape(-1, 128), "expert", axis=0, tiled=True)
    scores = scores.reshape(groups * exp_dev, slots)
    returned = lax.dynamic_slice_in_dim(scores, me * capacity, capacity, axis=1)
    every = jnp.arange(groups * exp_dev, dtype=jnp.int32)
    chose, _, put = slot_tables(expert_ids.T[None], every, capacity)
    by_token = jnp.sum(jnp.where(put[:, 0], returned[..., None], 0.0), axis=1)
    prob_grad = jnp.sum(jnp.where(chose[:, 0], by_token[:, None, :], 0.0), axis=0).T
    down_grad = jnp.sum(terms.astype(jnp.float32), axis=0)
    hidden_grad = hidden_grad.reshape(1, exp_dev, groups, capacity, hidden)
    return hidden_grad, prob_grad, down_grad[None]


def solution(mesh):
    tokens = P(("dp", "expert"), None)
    slots = P("dp", "expert", None, None, None)
    weights = P("expert", "dp", None)
    return jax.shard_map(
        on_device,
        mesh=mesh,
        in_specs=(tokens, tokens, tokens, slots, weights, P("expert")),
        out_specs=(slots, tokens, weights),
        check_vma=False,
    )
```

```python
import jax
import jax.numpy as jnp
from jax import lax
from jax.experimental import pallas as pl
from jax.experimental.pallas import tpu as pltpu
from jax.sharding import PartitionSpec as P

BATCH = 8
PACK = 4
SPAN = 512


def arrivals(chips):
    order = [0]
    for k in range(1, chips // 2):
        order += [k, -k]
    return order + [chips // 2]


def pack_kernel(*refs):
    *blocks, token_of, rows = refs
    experts, count, _ = token_of.shape
    part = count * PACK // BATCH
    tokens = jnp.concatenate([b[...] for b in blocks], axis=0)
    width = tokens.shape[0] * PACK // BATCH
    lanes = lax.broadcasted_iota(jnp.int32, (experts * part, width), 1)
    packed = []
    for h in range(BATCH // PACK):
        wanted = jnp.concatenate(
            [token_of[j, h * part:(h + 1) * part] for j in range(experts)], axis=0
        )
        packed.append(jnp.dot(
            (lanes == wanted).astype(jnp.bfloat16),
            tokens[h * width:(h + 1) * width],
            preferred_element_type=jnp.float32,
        ))
    for j in range(experts):
        rows[j] = jnp.concatenate(
            [p[j * part:(j + 1) * part] for p in packed], axis=0
        ).astype(jnp.bfloat16)


def pack(blocks, token_of):
    experts, count, _ = token_of.shape
    model = blocks[0].shape[1]
    width = sum(b.shape[0] for b in blocks)
    return pl.pallas_call(
        pack_kernel,
        grid=(model // SPAN,),
        in_specs=[pl.BlockSpec((b.shape[0], SPAN), lambda n: (0, n)) for b in blocks]
        + [pl.BlockSpec((experts, count, 1), lambda n: (0, 0, 0))],
        out_specs=pl.BlockSpec((experts, count, SPAN), lambda n: (0, 0, n)),
        out_shape=jax.ShapeDtypeStruct((experts, count, model), jnp.bfloat16),
        compiler_params=pltpu.CompilerParams(vmem_limit_bytes=40 << 20),
        cost_estimate=pl.CostEstimate(
            flops=experts * count * width * model,
            bytes_accessed=2 * (width + experts * count) * model,
            transcendentals=0,
        ),
    )(*blocks, token_of)


def term_kernel(flags, *refs):
    *pieces, weights, saved_t, term = refs
    any_trained = jnp.maximum(flags[0], flags[1]) > 0
    count = pieces[0].shape[1]
    scaled = [
        weights[0, i * count:(i + 1) * count] * p[0].astype(jnp.float32)
        for i, p in enumerate(pieces)
    ]
    scaled = jnp.where(any_trained, jnp.concatenate(scaled, axis=0), 0.0).astype(jnp.bfloat16)
    term[...] = jnp.dot(
        saved_t[...], scaled, preferred_element_type=jnp.float32
    ).astype(jnp.bfloat16)


def term_of(pieces, weights, saved_t, flags):
    _, count, model = pieces[0].shape
    hidden, slots = saved_t.shape

    def chosen(flags):
        return jnp.minimum(flags[1], 1)

    return pl.pallas_call(
        term_kernel,
        grid_spec=pltpu.PrefetchScalarGridSpec(
            num_scalar_prefetch=1,
            grid=(model // SPAN,),
            in_specs=[pl.BlockSpec((1, count, SPAN), lambda n, f: (chosen(f), 0, n)) for _ in pieces]
            + [
                pl.BlockSpec((1, slots, 1), lambda n, f: (chosen(f), 0, 0)),
                pl.BlockSpec((hidden, slots), lambda n, f: (0, 0)),
            ],
            out_specs=pl.BlockSpec((hidden, SPAN), lambda n, f: (0, n)),
        ),
        out_shape=jax.ShapeDtypeStruct((hidden, model), jnp.bfloat16),
        compiler_params=pltpu.CompilerParams(vmem_limit_bytes=40 << 20),
        cost_estimate=pl.CostEstimate(
            flops=2 * hidden * slots * model,
            bytes_accessed=2 * (slots + hidden) * model,
            transcendentals=0,
        ),
    )(flags, *pieces, weights, saved_t)


def grad_kernel(*refs):
    *pieces, weight, saved, weights, order, to_arrival, hidden, scores, arrived = refs
    count = pieces[0].shape[1]
    matrix = weight[:, 0].reshape(-1, weight.shape[-1])
    saved_now = jnp.dot(to_arrival[...], saved[0], preferred_element_type=jnp.float32)
    for i, p in enumerate(pieces):
        cut = slice(i * count, (i + 1) * count)
        grads = lax.dot_general(
            p[0], matrix, (((1,), (1,)), ((), ())), preferred_element_type=jnp.float32
        )
        arrived[cut] = (weights[0, cut] * grads).astype(jnp.bfloat16)
        scores[0, cut] = jnp.sum(grads * saved_now[cut], axis=1, keepdims=True)
    hidden[0] = jnp.dot(
        order[...], arrived[...], preferred_element_type=jnp.float32
    ).astype(jnp.bfloat16)


def grads_of(pieces, weight, saved, weights, order, to_arrival):
    _, count, model = pieces[0].shape
    experts, slots, hidden = saved.shape
    shards, _, shard, _ = weight.shape
    return pl.pallas_call(
        grad_kernel,
        grid=(experts,),
        in_specs=[pl.BlockSpec((1, count, model), lambda j: (j, 0, 0)) for _ in pieces]
        + [
            pl.BlockSpec((shards, 1, shard, model), lambda j: (0, j, 0, 0)),
            pl.BlockSpec((1, slots, hidden), lambda j: (j, 0, 0)),
            pl.BlockSpec((1, slots, 1), lambda j: (j, 0, 0)),
            pl.BlockSpec((slots, slots), lambda j: (0, 0)),
            pl.BlockSpec((slots, slots), lambda j: (0, 0)),
        ],
        out_specs=[
            pl.BlockSpec((1, slots, hidden), lambda j: (j, 0, 0)),
            pl.BlockSpec((1, slots, 1), lambda j: (j, 0, 0)),
        ],
        out_shape=[
            jax.ShapeDtypeStruct((experts, slots, hidden), jnp.bfloat16),
            jax.ShapeDtypeStruct((experts, slots, 1), jnp.float32),
        ],
        scratch_shapes=[pltpu.VMEM((slots, hidden), jnp.bfloat16)],
        compiler_params=pltpu.CompilerParams(vmem_limit_bytes=48 << 20),
        cost_estimate=pl.CostEstimate(
            flops=2 * experts * slots * hidden * (model + 2 * slots),
            bytes_accessed=2 * experts * (slots + hidden) * model + 4 * experts * slots * hidden,
            transcendentals=0,
        ),
    )(*pieces, weight, saved, weights, order, to_arrival)


def after(x, *others):
    zero = sum(o[(0,) * o.ndim].astype(jnp.float32) for o in others) * 0.0
    return x + zero.astype(x.dtype)


def slot_tables(ids, experts, capacity):
    named = ids[None] == experts[:, None, None, None]
    taken = jnp.any(named, axis=2)
    place = jnp.arange(ids.shape[-1], dtype=jnp.int32)
    earlier = (place[:, None] < place[None, :]).astype(jnp.bfloat16)
    rank = lax.dot_general(
        taken.astype(jnp.bfloat16), earlier, (((2,), (0,)), ((), ())),
        preferred_element_type=jnp.float32,
    ).astype(jnp.int32)
    each = jnp.arange(capacity, dtype=jnp.int32)[None, None, :, None]
    return named, taken, taken[:, :, None, :] & (rank[:, :, None, :] == each)


def on_device(upstream, expert_ids, route_probs, saved_hidden, down_weight, trained):
    tok_rows, model = upstream.shape
    top = expert_ids.shape[1]
    groups = lax.axis_size("expert")
    replicas = lax.axis_size("dp")
    chips = groups // 2
    exp_dev, shard, _ = down_weight.shape
    capacity, hidden = saved_hidden.shape[3:]
    slots = groups * capacity
    me = lax.axis_index("expert")
    chip, core = me // 2, me % 2

    def along(x, hops):
        return lax.ppermute(x, "expert", [(s, (s + 2 * hops) % groups) for s in range(groups)])

    def swap(x):
        return lax.ppermute(x, "expert", [(s, s ^ 1) for s in range(groups)])

    right, left = along(upstream, 1), along(upstream, -1)
    blocks = [upstream, left, right]

    routing = jnp.concatenate([expert_ids.T.astype(jnp.bfloat16), route_probs.T], axis=0)
    routing = lax.all_to_all(
        jnp.broadcast_to(routing[None], (groups, 2 * top, tok_rows)),
        "expert", split_axis=0, concat_axis=0, tiled=True,
    )

    weight = lax.all_to_all(
        jnp.broadcast_to(after(down_weight, routing)[None], (replicas, exp_dev, shard, model)),
        "dp", split_axis=0, concat_axis=0, tiled=True,
    )

    offsets = jnp.array(arrivals(chips), jnp.int32).reshape(-1, 1, BATCH)
    flips = jnp.arange(2, dtype=jnp.int32).reshape(1, 2, 1)
    source = ((chip + offsets) % chips * 2 + (core ^ flips)).reshape(-1)
    pick = (source[:, None] == jnp.arange(groups, dtype=jnp.int32)[None, :]).astype(jnp.bfloat16)
    routing = jnp.dot(
        pick, routing.reshape(groups, -1), preferred_element_type=jnp.float32
    ).reshape(groups, 2 * top, tok_rows)
    ids = routing[:, :top].astype(jnp.int32)
    probs = routing[:, top:]
    mine = me * exp_dev + jnp.arange(exp_dev, dtype=jnp.int32)
    theirs = (me ^ 1) * exp_dev + jnp.arange(exp_dev, dtype=jnp.int32)
    named, _, at_mine = slot_tables(ids, mine, capacity)
    prob_of = jnp.sum(jnp.where(named, probs[None], 0.0), axis=2)
    slot_prob = jnp.sum(jnp.where(at_mine, prob_of[:, :, None, :], 0.0), axis=3)
    slot_prob = slot_prob.reshape(exp_dev, slots, 1)

    def same_core(x):
        return x.reshape(x.shape[0], -1, 2, BATCH, *x.shape[2:])[:, :, 0]

    same_ids = ids.reshape(-1, 2, BATCH, top, tok_rows)[:, 0].reshape(-1, top, tok_rows)
    at_theirs = slot_tables(same_ids, theirs, capacity)[2]
    at_theirs = at_theirs.reshape(exp_dev, -1, BATCH, capacity, tok_rows)
    place = jnp.arange(tok_rows, dtype=jnp.int32)
    local = (jnp.arange(BATCH, dtype=jnp.int32) % PACK)[:, None] * tok_rows + place[None, :]

    def token_table(at):
        table = jnp.max(jnp.where(at, local[None, None, :, None, :], -1), axis=4)
        return table.reshape(exp_dev, -1, BATCH * capacity, 1)

    for_mine, for_theirs = token_table(same_core(at_mine)), token_table(at_theirs)

    target = (jnp.arange(capacity, dtype=jnp.int32)[None, :] * groups + source[:, None]).reshape(-1)
    index = jnp.arange(slots, dtype=jnp.int32)
    order = (target[None, :] == index[:, None]).astype(jnp.bfloat16)
    to_arrival = (target[:, None] == index[None, :]).astype(jnp.bfloat16)
    saved = saved_hidden[0].transpose(0, 2, 1, 3).reshape(exp_dev, slots, hidden)
    saved_t = lax.dot_general(
        jnp.where(trained[1] > 0, saved[1], saved[0]), order, (((0,), (0,)), ((), ())),
        preferred_element_type=jnp.float32,
    ).astype(jnp.bfloat16)

    pieces = []
    half = tok_rows // 2
    for k in range(2, chips // 2 + 1):
        if k == chips // 2:
            blocks += [along(right[:half], 1), along(left[half:], -1)]
        else:
            right, left = along(right, 1), along(left, -1)
            blocks += [left, right]
        if k == 2:
            left, right = after(left, right), after(right, left)
        while len(pieces) < 2 * (chips // BATCH) and (
            len(blocks) >= len(pieces) // 2 * BATCH + BATCH + 2 or k == chips // 2
        ):
            b = len(pieces) // 2
            last = b == chips // BATCH - 1
            batch = blocks[b * BATCH:] if last else blocks[b * BATCH:(b + 1) * BATCH]
            packed = pack(batch, for_theirs[:, b])
            pieces += [pack(batch, for_mine[:, b]), swap(packed)]
            if not last:
                left = after(left, packed, pieces[-2])
                right = after(right, packed, saved_t, slot_prob)

    term = term_of(pieces, slot_prob, saved_t, trained)
    terms = lax.all_to_all(
        term.reshape(replicas, shard, model), "dp", split_axis=0, concat_axis=0, tiled=True
    )
    hidden_grad, scores = grads_of(pieces, weight, saved, slot_prob, order, to_arrival)
    hidden_grad = hidden_grad.reshape(exp_dev, capacity, groups, hidden).transpose(0, 2, 1, 3)

    scores = lax.all_gather(scores.reshape(1, -1), "expert", axis=0, tiled=True)
    scores = scores.reshape(groups, exp_dev, groups, capacity)
    owner = jnp.arange(groups, dtype=jnp.int32)[:, None, None, None]
    flat = jnp.broadcast_to(offsets, (chips // BATCH, 2, BATCH))
    from_owner = ((owner // 2 + flat[None]) % chips * 2 + (owner % 2 ^ flips[None])) == me
    from_owner = from_owner.reshape(groups, 1, groups, 1)
    returned = jnp.sum(jnp.where(from_owner, scores, 0.0), axis=2).reshape(groups * exp_dev, capacity)
    every = jnp.arange(groups * exp_dev, dtype=jnp.int32)
    chose, _, put = slot_tables(expert_ids.T[None], every, capacity)
    by_token = jnp.sum(jnp.where(put[:, 0], returned[..., None], 0.0), axis=1)
    prob_grad = jnp.sum(jnp.where(chose[:, 0], by_token[:, None, :], 0.0), axis=0).T
    down_grad = jnp.sum(terms.astype(jnp.float32), axis=0)
    return hidden_grad[None], prob_grad, down_grad[None]


def solution(mesh):
    tokens = P(("dp", "expert"), None)
    slots = P("dp", "expert", None, None, None)
    weights = P("expert", "dp", None)
    return jax.shard_map(
        on_device,
        mesh=mesh,
        in_specs=(tokens, tokens, tokens, slots, weights, P("expert")),
        out_specs=(slots, tokens, weights),
        check_vma=False,
    )
```

```python
import jax
import jax.numpy as jnp
from jax import lax
from jax.experimental import pallas as pl
from jax.experimental.pallas import tpu as pltpu
from jax.sharding import PartitionSpec as P

PACK = 4
SPAN = 256


def pack_kernel(trained, tokens, token_of, weights, saved_t, *others):
    rows, term = others[-2:]
    experts, slots, _ = token_of.shape
    packs = tokens.shape[0] // (PACK * 128)
    part = slots // packs
    width = PACK * 128
    lanes = lax.broadcasted_iota(jnp.int32, (experts * part, width), 1)
    blocks = []
    for q in range(packs):
        wanted = jnp.concatenate(
            [token_of[j, q * part:(q + 1) * part] for j in range(experts)], axis=0
        )
        blocks.append(jnp.dot(
            (lanes == wanted).astype(jnp.bfloat16),
            tokens[q * width:(q + 1) * width],
            preferred_element_type=jnp.float32,
        ))
    packed = [
        jnp.concatenate([b[j * part:(j + 1) * part] for b in blocks], axis=0) for j in range(experts)
    ]
    for j in range(experts):
        rows[j] = packed[j].astype(jnp.bfloat16)
    chosen = jnp.where(trained[1] > 0, packed[1], packed[0])
    scaled = (weights[...] * chosen).astype(jnp.bfloat16)
    term[...] = jnp.dot(
        saved_t[...], scaled, preferred_element_type=jnp.float32
    ).astype(jnp.bfloat16)


def pack(tokens, token_of, weights, saved_t, trained, *later):
    count, model = tokens.shape
    experts, slots, _ = token_of.shape
    hidden = saved_t.shape[0]
    return pl.pallas_call(
        pack_kernel,
        grid=(model // SPAN,),
        in_specs=[
            pl.BlockSpec(memory_space=pltpu.SMEM),
            pl.BlockSpec((count, SPAN), lambda n: (0, n)),
            pl.BlockSpec((experts, slots, 1), lambda n: (0, 0, 0)),
            pl.BlockSpec((slots, 1), lambda n: (0, 0)),
            pl.BlockSpec((hidden, slots), lambda n: (0, 0)),
            *[pl.BlockSpec(memory_space=pl.ANY) for _ in later],
        ],
        out_specs=[
            pl.BlockSpec((experts, slots, SPAN), lambda n: (0, 0, n)),
            pl.BlockSpec((hidden, SPAN), lambda n: (0, n)),
        ],
        out_shape=[
            pltpu.HBM((experts, slots, model), jnp.bfloat16),
            pltpu.HBM((hidden, model), jnp.bfloat16),
        ],
        compiler_params=pltpu.CompilerParams(vmem_limit_bytes=40 << 20),
        cost_estimate=pl.CostEstimate(
            flops=2 * experts * slots * PACK * 128 * model + 2 * hidden * slots * model,
            bytes_accessed=2 * (count + experts * slots + hidden) * model,
            transcendentals=0,
        ),
    )(trained, tokens, token_of, weights, saved_t, *later)


def grad_kernel(rows, weight, saved, probs, order, to_source, hidden, scores):
    grads = lax.dot_general(
        rows[0],
        weight[:, 0].reshape(-1, weight.shape[-1]),
        (((1,), (1,)), ((), ())),
        preferred_element_type=jnp.float32,
    )
    width = grads.shape[1]
    saved_now = jnp.dot(
        to_source[...], saved[0].reshape(-1, width), preferred_element_type=jnp.float32
    )
    scores[0] = jnp.sum(grads * saved_now, axis=1, keepdims=True)
    scaled = (probs[0] * grads).astype(jnp.bfloat16)
    hidden[0] = jnp.dot(
        order[...], scaled, preferred_element_type=jnp.float32
    ).astype(jnp.bfloat16).reshape(hidden.shape[1:])


def half_orders(groups, capacity):
    some = groups // 2
    index = jnp.arange(some * capacity, dtype=jnp.int32)
    place = index % capacity * some + index // capacity
    order = place[None, :] == index[:, None]
    return order.astype(jnp.bfloat16), order.T.astype(jnp.bfloat16)


def grads_of(rows, weight, saved, probs, order, to_source):
    experts, slots, model = rows.shape
    _, capacity, groups, hidden = saved.shape
    halves = 2
    part, some = slots // halves, groups // halves
    shards, _, shard, _ = weight.shape
    return pl.pallas_call(
        grad_kernel,
        grid=(experts, halves),
        in_specs=[
            pl.BlockSpec((1, part, model), lambda j, i: (j, i, 0)),
            pl.BlockSpec((shards, 1, shard, model), lambda j, i: (0, j, 0, 0)),
            pl.BlockSpec((1, capacity, some, hidden), lambda j, i: (j, 0, i, 0)),
            pl.BlockSpec((1, part, 1), lambda j, i: (j, i, 0)),
            pl.BlockSpec((part, part), lambda j, i: (0, 0)),
            pl.BlockSpec((part, part), lambda j, i: (0, 0)),
        ],
        out_specs=[
            pl.BlockSpec((1, capacity, some, hidden), lambda j, i: (j, 0, i, 0)),
            pl.BlockSpec((1, part, 1), lambda j, i: (j, i, 0)),
        ],
        out_shape=[
            jax.ShapeDtypeStruct(saved.shape, jnp.bfloat16),
            jax.ShapeDtypeStruct((experts, slots, 1), jnp.float32),
        ],
        compiler_params=pltpu.CompilerParams(vmem_limit_bytes=48 << 20),
        cost_estimate=pl.CostEstimate(
            flops=2 * experts * slots * hidden * (model + 2 * part),
            bytes_accessed=2 * experts * (slots + hidden) * model + 4 * experts * slots * hidden,
            transcendentals=0,
        ),
    )(rows, weight, saved, probs, order, to_source)


def total_kernel(terms, total):
    total[...] = jnp.sum(terms[...].astype(jnp.float32), axis=0)


def total_of(terms):
    replicas, shard, model = terms.shape
    span = 512
    return pl.pallas_call(
        total_kernel,
        grid=(model // span,),
        in_specs=[pl.BlockSpec((replicas, shard, span), lambda n: (0, 0, n))],
        out_specs=pl.BlockSpec((shard, span), lambda n: (0, n)),
        out_shape=jax.ShapeDtypeStruct((shard, model), jnp.float32),
        cost_estimate=pl.CostEstimate(
            flops=replicas * shard * model,
            bytes_accessed=(2 * replicas + 4) * shard * model,
            transcendentals=0,
        ),
    )(terms)


def ranks_of(ids, experts):
    named = ids[None] == experts[:, None, None, None]
    taken = jnp.any(named, axis=2)
    place = jnp.arange(ids.shape[-1], dtype=jnp.int32)
    earlier = (place[:, None] < place[None, :]).astype(jnp.bfloat16)
    rank = lax.dot_general(
        taken.astype(jnp.bfloat16), earlier, (((2,), (0,)), ((), ())),
        preferred_element_type=jnp.float32,
    ).astype(jnp.int32)
    return named, taken, rank


def on_device(upstream, expert_ids, route_probs, saved_hidden, down_weight, trained):
    tok_rows, model = upstream.shape
    top = expert_ids.shape[1]
    groups = lax.axis_size("expert")
    replicas = lax.axis_size("dp")
    exp_dev, shard, _ = down_weight.shape
    capacity, hidden = saved_hidden.shape[3:]
    slots = groups * capacity

    tokens = lax.all_gather(upstream, "expert", axis=0, tiled=True)

    weight = lax.all_to_all(
        jnp.broadcast_to(down_weight[None], (replicas, exp_dev, shard, model)),
        "dp", split_axis=0, concat_axis=0, tiled=True,
    )

    routing = jnp.concatenate([expert_ids.T.astype(jnp.bfloat16), route_probs.T], axis=0)
    routing = lax.all_gather(routing, "expert", axis=0, tiled=True)
    routing = routing.reshape(groups, 2 * top, tok_rows)
    ids = routing[:, :top].astype(jnp.int32)
    probs = routing[:, top:].astype(jnp.float32)
    me = lax.axis_index("expert")
    own = me * exp_dev + jnp.arange(exp_dev, dtype=jnp.int32)
    named, taken, rank = ranks_of(ids, own)
    at_slot = taken[:, :, None, :] & (
        rank[:, :, None, :] == jnp.arange(capacity, dtype=jnp.int32)[None, None, :, None]
    )
    prob_of = jnp.sum(jnp.where(named, probs[None], 0.0), axis=2)
    place = jnp.arange(tok_rows, dtype=jnp.int32)
    local = (jnp.arange(groups, dtype=jnp.int32) % PACK)[:, None] * tok_rows + place[None, :]
    token_of = jnp.max(jnp.where(at_slot, local[None, :, None, :], -1), axis=3)
    slot_prob = jnp.sum(jnp.where(at_slot, prob_of[:, :, None, :], 0.0), axis=3)
    token_of = token_of.reshape(exp_dev, slots, 1)
    slot_prob = slot_prob.reshape(exp_dev, slots, 1)

    saved_t = jnp.where(trained[1] > 0, saved_hidden[0, 1], saved_hidden[0, 0])
    saved_t = saved_t.reshape(slots, hidden).T
    term_prob = jnp.where(trained[1] > 0, slot_prob[1], slot_prob[0])
    term_prob = jnp.where(jnp.max(trained) > 0, term_prob, 0.0)

    every = jnp.arange(groups * exp_dev, dtype=jnp.int32)
    chose, own_taken, own_rank = ranks_of(expert_ids.T[None], every)
    own_slot = jnp.where(own_taken, own_rank, -1)[:, 0]
    order, to_source = half_orders(groups, capacity)

    rows, term = pack(
        tokens, token_of, term_prob, saved_t, trained, slot_prob, order, to_source, own_slot
    )
    terms = lax.all_to_all(
        term.reshape(replicas, shard, model), "dp", split_axis=0, concat_axis=0, tiled=True
    )
    saved = saved_hidden[0].transpose(0, 2, 1, 3)
    hidden_grad, scores = grads_of(rows, weight, saved, slot_prob, order, to_source)
    scores = lax.all_gather(scores.reshape(-1, 128), "expert", axis=0, tiled=True)
    scores = scores.reshape(groups * exp_dev, slots)
    returned = lax.dynamic_slice_in_dim(scores, me * capacity, capacity, axis=1)
    put = own_slot[:, None, :] == jnp.arange(capacity, dtype=jnp.int32)[None, :, None]
    by_token = jnp.sum(jnp.where(put, returned[..., None], 0.0), axis=1)
    prob_grad = jnp.sum(jnp.where(chose[:, 0], by_token[:, None, :], 0.0), axis=0).T
    down_grad = total_of(terms)
    return hidden_grad.transpose(0, 2, 1, 3)[None], prob_grad, down_grad[None]


def solution(mesh):
    tokens = P(("dp", "expert"), None)
    slots = P("dp", "expert", None, None, None)
    weights = P("expert", "dp", None)
    return jax.shard_map(
        on_device,
        mesh=mesh,
        in_specs=(tokens, tokens, tokens, slots, weights, P("expert")),
        out_specs=(slots, tokens, weights),
        check_vma=False,
    )
```

```python
import jax
import jax.numpy as jnp
from jax import lax
from jax.experimental import pallas as pl
from jax.experimental.pallas import tpu as pltpu
from jax.sharding import PartitionSpec as P

PACK = 4
SPAN = 512


def pack_kernel(trained, tokens, token_of, weights, saved_t, *others):
    rows, term = others[-2:]
    experts, slots, _ = token_of.shape
    packs = tokens.shape[0] // (PACK * 128)
    part = slots // packs
    width = PACK * 128
    lanes = lax.broadcasted_iota(jnp.int32, (experts * part, width), 1)
    blocks = []
    for q in range(packs):
        wanted = jnp.concatenate(
            [token_of[j, q * part:(q + 1) * part] for j in range(experts)], axis=0
        )
        blocks.append(jnp.dot(
            (lanes == wanted).astype(jnp.bfloat16),
            tokens[q * width:(q + 1) * width],
            preferred_element_type=jnp.float32,
        ))
    packed = [
        jnp.concatenate([b[j * part:(j + 1) * part] for b in blocks], axis=0) for j in range(experts)
    ]
    for j in range(experts):
        rows[j] = packed[j].astype(jnp.bfloat16)
    chosen = jnp.where(trained[1] > 0, packed[1], packed[0])
    scaled = (weights[...] * chosen).astype(jnp.bfloat16)
    term[...] = jnp.dot(
        saved_t[...], scaled, preferred_element_type=jnp.float32
    ).astype(jnp.bfloat16)


def pack(tokens, token_of, weights, saved_t, trained, *later):
    count, model = tokens.shape
    experts, slots, _ = token_of.shape
    hidden = saved_t.shape[0]
    return pl.pallas_call(
        pack_kernel,
        grid=(model // SPAN,),
        in_specs=[
            pl.BlockSpec(memory_space=pltpu.SMEM),
            pl.BlockSpec((count, SPAN), lambda n: (0, n)),
            pl.BlockSpec((experts, slots, 1), lambda n: (0, 0, 0)),
            pl.BlockSpec((slots, 1), lambda n: (0, 0)),
            pl.BlockSpec((hidden, slots), lambda n: (0, 0)),
            *[pl.BlockSpec(memory_space=pl.ANY) for _ in later],
        ],
        out_specs=[
            pl.BlockSpec((experts, slots, SPAN), lambda n: (0, 0, n)),
            pl.BlockSpec((hidden, SPAN), lambda n: (0, n)),
        ],
        out_shape=[
            pltpu.HBM((experts, slots, model), jnp.bfloat16),
            pltpu.HBM((hidden, model), jnp.bfloat16),
        ],
        compiler_params=pltpu.CompilerParams(vmem_limit_bytes=24 << 20),
        cost_estimate=pl.CostEstimate(
            flops=2 * experts * slots * PACK * 128 * model + 2 * hidden * slots * model,
            bytes_accessed=2 * (count + experts * slots + hidden) * model,
            transcendentals=0,
        ),
    )(trained, tokens, token_of, weights, saved_t, *later)


def grad_kernel(rows, weight, saved, probs, order, to_source, hidden, scores):
    grads = lax.dot_general(
        rows[0],
        weight[:, 0].reshape(-1, weight.shape[-1]),
        (((1,), (1,)), ((), ())),
        preferred_element_type=jnp.float32,
    )
    width = grads.shape[1]
    saved_now = jnp.dot(
        to_source[...], saved[0].reshape(-1, width), preferred_element_type=jnp.float32
    )
    scores[0] = jnp.sum(grads * saved_now, axis=1, keepdims=True)
    scaled = (probs[0] * grads).astype(jnp.bfloat16)
    hidden[0] = jnp.dot(
        order[...], scaled, preferred_element_type=jnp.float32
    ).astype(jnp.bfloat16).reshape(hidden.shape[1:])


def half_orders(groups, capacity):
    some = groups // 2
    index = jnp.arange(some * capacity, dtype=jnp.int32)
    place = index % capacity * some + index // capacity
    order = place[None, :] == index[:, None]
    return order.astype(jnp.bfloat16), order.T.astype(jnp.bfloat16)


def grads_of(rows, weight, saved, probs, order, to_source):
    experts, slots, model = rows.shape
    _, capacity, groups, hidden = saved.shape
    halves = 2
    part, some = slots // halves, groups // halves
    shards, _, shard, _ = weight.shape
    return pl.pallas_call(
        grad_kernel,
        grid=(experts, halves),
        in_specs=[
            pl.BlockSpec((1, part, model), lambda j, i: (j, i, 0)),
            pl.BlockSpec((shards, 1, shard, model), lambda j, i: (0, j, 0, 0)),
            pl.BlockSpec((1, capacity, some, hidden), lambda j, i: (j, 0, i, 0)),
            pl.BlockSpec((1, part, 1), lambda j, i: (j, i, 0)),
            pl.BlockSpec((part, part), lambda j, i: (0, 0)),
            pl.BlockSpec((part, part), lambda j, i: (0, 0)),
        ],
        out_specs=[
            pl.BlockSpec((1, capacity, some, hidden), lambda j, i: (j, 0, i, 0)),
            pl.BlockSpec((1, part, 1), lambda j, i: (j, i, 0)),
        ],
        out_shape=[
            jax.ShapeDtypeStruct(saved.shape, jnp.bfloat16),
            jax.ShapeDtypeStruct((experts, slots, 1), jnp.float32),
        ],
        compiler_params=pltpu.CompilerParams(vmem_limit_bytes=24 << 20),
        cost_estimate=pl.CostEstimate(
            flops=2 * experts * slots * hidden * (model + 2 * part),
            bytes_accessed=2 * experts * (slots + hidden) * model + 4 * experts * slots * hidden,
            transcendentals=0,
        ),
    )(rows, weight, saved, probs, order, to_source)


def total_kernel(*refs):
    *terms, total = refs
    total[...] = sum(jnp.sum(t[...].astype(jnp.float32), axis=0) for t in terms)


def total_of(terms):
    replicas, shard, model = terms.shape
    span, cuts = model // 2, 4
    return pl.pallas_call(
        total_kernel,
        grid=(model // span,),
        in_specs=[
            pl.BlockSpec((replicas // cuts, shard, span), lambda n, q=q: (q, 0, n))
            for q in range(cuts)
        ],
        out_specs=pl.BlockSpec((shard, span), lambda n: (0, n)),
        out_shape=jax.ShapeDtypeStruct((shard, model), jnp.float32),
        cost_estimate=pl.CostEstimate(
            flops=replicas * shard * model,
            bytes_accessed=(2 * replicas + 4) * shard * model,
            transcendentals=0,
        ),
    )(*[terms] * cuts)


def ranks_of(ids, experts):
    named = ids[None] == experts[:, None, None, None]
    taken = jnp.any(named, axis=2)
    place = jnp.arange(ids.shape[-1], dtype=jnp.int32)
    earlier = (place[:, None] < place[None, :]).astype(jnp.bfloat16)
    rank = lax.dot_general(
        taken.astype(jnp.bfloat16), earlier, (((2,), (0,)), ((), ())),
        preferred_element_type=jnp.float32,
    ).astype(jnp.int32)
    return named, taken, rank


def on_device(upstream, expert_ids, route_probs, saved_hidden, down_weight, trained):
    tok_rows, model = upstream.shape
    top = expert_ids.shape[1]
    groups = lax.axis_size("expert")
    replicas = lax.axis_size("dp")
    exp_dev, shard, _ = down_weight.shape
    capacity, hidden = saved_hidden.shape[3:]
    slots = groups * capacity

    tokens = lax.all_gather(upstream, "expert", axis=0, tiled=True)

    weight = lax.all_to_all(
        jnp.broadcast_to(down_weight[None], (replicas, exp_dev, shard, model)),
        "dp", split_axis=0, concat_axis=0, tiled=True,
    )

    routing = jnp.concatenate([expert_ids.T.astype(jnp.bfloat16), route_probs.T], axis=0)
    routing = lax.all_gather(routing, "expert", axis=0, tiled=True)
    routing = routing.reshape(groups, 2 * top, tok_rows)
    ids = routing[:, :top].astype(jnp.int32)
    probs = routing[:, top:].astype(jnp.float32)
    me = lax.axis_index("expert")
    own = me * exp_dev + jnp.arange(exp_dev, dtype=jnp.int32)
    named, taken, rank = ranks_of(ids, own)
    at_slot = taken[:, :, None, :] & (
        rank[:, :, None, :] == jnp.arange(capacity, dtype=jnp.int32)[None, None, :, None]
    )
    prob_of = jnp.sum(jnp.where(named, probs[None], 0.0), axis=2)
    place = jnp.arange(tok_rows, dtype=jnp.int32)
    local = (jnp.arange(groups, dtype=jnp.int32) % PACK)[:, None] * tok_rows + place[None, :]
    token_of = jnp.max(jnp.where(at_slot, local[None, :, None, :], -1), axis=3)
    slot_prob = jnp.sum(jnp.where(at_slot, prob_of[:, :, None, :], 0.0), axis=3)
    token_of = token_of.reshape(exp_dev, slots, 1)
    slot_prob = slot_prob.reshape(exp_dev, slots, 1)

    saved_t = jnp.where(trained[1] > 0, saved_hidden[0, 1], saved_hidden[0, 0])
    saved_t = saved_t.reshape(slots, hidden).T
    term_prob = jnp.where(trained[1] > 0, slot_prob[1], slot_prob[0])
    term_prob = jnp.where(jnp.max(trained) > 0, term_prob, 0.0)

    every = jnp.arange(groups * exp_dev, dtype=jnp.int32)
    chose, own_taken, own_rank = ranks_of(expert_ids.T[None], every)
    own_slot = jnp.where(own_taken, own_rank, -1)[:, 0]
    order, to_source = half_orders(groups, capacity)

    rows, term = pack(
        tokens, token_of, term_prob, saved_t, trained, slot_prob, order, to_source, own_slot
    )
    terms = lax.all_to_all(
        term.reshape(replicas, shard, model), "dp", split_axis=0, concat_axis=0, tiled=True
    )
    saved = saved_hidden[0].transpose(0, 2, 1, 3)
    hidden_grad, scores = grads_of(rows, weight, saved, slot_prob, order, to_source)
    scores = lax.all_gather(scores.reshape(-1, 128), "expert", axis=0, tiled=True)
    scores = scores.reshape(groups * exp_dev, slots)
    returned = lax.dynamic_slice_in_dim(scores, me * capacity, capacity, axis=1)
    put = own_slot[:, None, :] == jnp.arange(capacity, dtype=jnp.int32)[None, :, None]
    by_token = jnp.sum(jnp.where(put, returned[..., None], 0.0), axis=1)
    prob_grad = jnp.sum(jnp.where(chose[:, 0], by_token[:, None, :], 0.0), axis=0).T
    down_grad = total_of(terms)
    return hidden_grad.transpose(0, 2, 1, 3)[None], prob_grad, down_grad[None]


def solution(mesh):
    tokens = P(("dp", "expert"), None)
    slots = P("dp", "expert", None, None, None)
    weights = P("expert", "dp", None)
    return jax.shard_map(
        on_device,
        mesh=mesh,
        in_specs=(tokens, tokens, tokens, slots, weights, P("expert")),
        out_specs=(slots, tokens, weights),
        check_vma=False,
    )
```

```python
import jax
import jax.numpy as jnp
from jax import lax
from jax.experimental import pallas as pl
from jax.experimental.pallas import tpu as pltpu
from jax.sharding import PartitionSpec as P

PACK = 4
SPAN = 1024


def pack_kernel(trained, tokens, token_of, weights, saved_t, *others):
    rows, term = others[-2:]
    experts, slots, _ = token_of.shape
    packs = tokens.shape[0] // (PACK * 128)
    part = slots // packs
    width = PACK * 128
    lanes = lax.broadcasted_iota(jnp.int32, (experts * part, width), 1)
    blocks = []
    for q in range(packs):
        wanted = jnp.concatenate(
            [token_of[j, q * part:(q + 1) * part] for j in range(experts)], axis=0
        )
        blocks.append(jnp.dot(
            (lanes == wanted).astype(jnp.bfloat16),
            tokens[q * width:(q + 1) * width],
            preferred_element_type=jnp.float32,
        ))
    packed = [
        jnp.concatenate([b[j * part:(j + 1) * part] for b in blocks], axis=0) for j in range(experts)
    ]
    for j in range(experts):
        rows[j] = packed[j].astype(jnp.bfloat16)
    chosen = jnp.where(trained[1] > 0, packed[1], packed[0])
    scaled = (weights[...] * chosen).astype(jnp.bfloat16)
    term[...] = jnp.dot(
        saved_t[...], scaled, preferred_element_type=jnp.float32
    ).astype(jnp.bfloat16)


def pack(tokens, token_of, weights, saved_t, trained, *later):
    count, model = tokens.shape
    experts, slots, _ = token_of.shape
    hidden = saved_t.shape[0]
    return pl.pallas_call(
        pack_kernel,
        grid=(model // SPAN,),
        in_specs=[
            pl.BlockSpec(memory_space=pltpu.SMEM),
            pl.BlockSpec((count, SPAN), lambda n: (0, n)),
            pl.BlockSpec((experts, slots, 1), lambda n: (0, 0, 0)),
            pl.BlockSpec((slots, 1), lambda n: (0, 0)),
            pl.BlockSpec((hidden, slots), lambda n: (0, 0)),
            *[pl.BlockSpec(memory_space=pl.ANY) for _ in later],
        ],
        out_specs=[
            pl.BlockSpec((experts, slots, SPAN), lambda n: (0, 0, n)),
            pl.BlockSpec((hidden, SPAN), lambda n: (0, n)),
        ],
        out_shape=[
            pltpu.HBM((experts, slots, model), jnp.bfloat16),
            pltpu.HBM((hidden, model), jnp.bfloat16),
        ],
        compiler_params=pltpu.CompilerParams(vmem_limit_bytes=48 << 20),
        cost_estimate=pl.CostEstimate(
            flops=2 * experts * slots * PACK * 128 * model + 2 * hidden * slots * model,
            bytes_accessed=2 * (count + experts * slots + hidden) * model,
            transcendentals=0,
        ),
    )(trained, tokens, token_of, weights, saved_t, *later)


def grad_kernel(rows, weight, saved, probs, order, to_source, hidden, scores):
    grads = lax.dot_general(
        rows[0],
        weight[:, 0].reshape(-1, weight.shape[-1]),
        (((1,), (1,)), ((), ())),
        preferred_element_type=jnp.float32,
    )
    width = grads.shape[1]
    saved_now = jnp.dot(
        to_source[...], saved[0].reshape(-1, width), preferred_element_type=jnp.float32
    )
    scores[0] = jnp.sum(grads * saved_now, axis=1, keepdims=True)
    scaled = (probs[0] * grads).astype(jnp.bfloat16)
    hidden[0] = jnp.dot(
        order[...], scaled, preferred_element_type=jnp.float32
    ).astype(jnp.bfloat16).reshape(hidden.shape[1:])


def half_orders(groups, capacity):
    some = groups // 2
    index = jnp.arange(some * capacity, dtype=jnp.int32)
    place = index % capacity * some + index // capacity
    order = place[None, :] == index[:, None]
    return order.astype(jnp.bfloat16), order.T.astype(jnp.bfloat16)


def grads_of(rows, weight, saved, probs, order, to_source):
    experts, slots, model = rows.shape
    _, capacity, groups, hidden = saved.shape
    halves = 2
    part, some = slots // halves, groups // halves
    shards, _, shard, _ = weight.shape
    return pl.pallas_call(
        grad_kernel,
        grid=(experts, halves),
        in_specs=[
            pl.BlockSpec((1, part, model), lambda j, i: (j, i, 0)),
            pl.BlockSpec((shards, 1, shard, model), lambda j, i: (0, j, 0, 0)),
            pl.BlockSpec((1, capacity, some, hidden), lambda j, i: (j, 0, i, 0)),
            pl.BlockSpec((1, part, 1), lambda j, i: (j, i, 0)),
            pl.BlockSpec((part, part), lambda j, i: (0, 0)),
            pl.BlockSpec((part, part), lambda j, i: (0, 0)),
        ],
        out_specs=[
            pl.BlockSpec((1, capacity, some, hidden), lambda j, i: (j, 0, i, 0)),
            pl.BlockSpec((1, part, 1), lambda j, i: (j, i, 0)),
        ],
        out_shape=[
            jax.ShapeDtypeStruct(saved.shape, jnp.bfloat16),
            jax.ShapeDtypeStruct((experts, slots, 1), jnp.float32),
        ],
        compiler_params=pltpu.CompilerParams(vmem_limit_bytes=48 << 20),
        cost_estimate=pl.CostEstimate(
            flops=2 * experts * slots * hidden * (model + 2 * part),
            bytes_accessed=2 * experts * (slots + hidden) * model + 4 * experts * slots * hidden,
            transcendentals=0,
        ),
    )(rows, weight, saved, probs, order, to_source)


def total_kernel(*refs):
    *terms, total = refs
    total[...] = sum(jnp.sum(t[...].astype(jnp.float32), axis=0) for t in terms)


def total_of(terms):
    replicas, shard, model = terms.shape
    span, cuts = model // 2, min(4, replicas)
    return pl.pallas_call(
        total_kernel,
        grid=(model // span,),
        in_specs=[
            pl.BlockSpec((replicas // cuts, shard, span), lambda n, q=q: (q, 0, n))
            for q in range(cuts)
        ],
        out_specs=pl.BlockSpec((shard, span), lambda n: (0, n)),
        out_shape=jax.ShapeDtypeStruct((shard, model), jnp.float32),
        cost_estimate=pl.CostEstimate(
            flops=replicas * shard * model,
            bytes_accessed=(2 * replicas + 4) * shard * model,
            transcendentals=0,
        ),
    )(*[terms] * cuts)


def ranks_of(ids, experts):
    named = ids[None] == experts[:, None, None, None]
    taken = jnp.any(named, axis=2)
    place = jnp.arange(ids.shape[-1], dtype=jnp.int32)
    earlier = (place[:, None] < place[None, :]).astype(jnp.bfloat16)
    rank = lax.dot_general(
        taken.astype(jnp.bfloat16), earlier, (((2,), (0,)), ((), ())),
        preferred_element_type=jnp.float32,
    ).astype(jnp.int32)
    return named, taken, rank


def on_device(upstream, expert_ids, route_probs, saved_hidden, down_weight, trained):
    tok_rows, model = upstream.shape
    top = expert_ids.shape[1]
    groups = lax.axis_size("expert")
    replicas = lax.axis_size("dp")
    exp_dev, shard, _ = down_weight.shape
    capacity, hidden = saved_hidden.shape[3:]
    slots = groups * capacity

    tokens = lax.all_gather(upstream, "expert", axis=0, tiled=True)

    weight = lax.all_to_all(
        jnp.broadcast_to(down_weight[None], (replicas, exp_dev, shard, model)),
        "dp", split_axis=0, concat_axis=0, tiled=True,
    )

    routing = jnp.concatenate([expert_ids.T.astype(jnp.bfloat16), route_probs.T], axis=0)
    routing = lax.all_gather(routing, "expert", axis=0, tiled=True)
    routing = routing.reshape(groups, 2 * top, tok_rows)
    ids = routing[:, :top].astype(jnp.int32)
    probs = routing[:, top:].astype(jnp.float32)
    me = lax.axis_index("expert")
    own = me * exp_dev + jnp.arange(exp_dev, dtype=jnp.int32)
    named, taken, rank = ranks_of(ids, own)
    at_slot = taken[:, :, None, :] & (
        rank[:, :, None, :] == jnp.arange(capacity, dtype=jnp.int32)[None, None, :, None]
    )
    prob_of = jnp.sum(jnp.where(named, probs[None], 0.0), axis=2)
    place = jnp.arange(tok_rows, dtype=jnp.int32)
    local = (jnp.arange(groups, dtype=jnp.int32) % PACK)[:, None] * tok_rows + place[None, :]
    token_of = jnp.max(jnp.where(at_slot, local[None, :, None, :], -1), axis=3)
    slot_prob = jnp.sum(jnp.where(at_slot, prob_of[:, :, None, :], 0.0), axis=3)
    token_of = token_of.reshape(exp_dev, slots, 1)
    slot_prob = slot_prob.reshape(exp_dev, slots, 1)

    saved_t = jnp.where(trained[1] > 0, saved_hidden[0, 1], saved_hidden[0, 0])
    saved_t = saved_t.reshape(slots, hidden).T
    term_prob = jnp.where(trained[1] > 0, slot_prob[1], slot_prob[0])
    term_prob = jnp.where(jnp.max(trained) > 0, term_prob, 0.0)

    every = jnp.arange(groups * exp_dev, dtype=jnp.int32)
    chose, own_taken, own_rank = ranks_of(expert_ids.T[None], every)
    own_slot = jnp.where(own_taken, own_rank, -1)[:, 0]
    order, to_source = half_orders(groups, capacity)

    rows, term = pack(
        tokens, token_of, term_prob, saved_t, trained, slot_prob, order, to_source, own_slot
    )
    terms = lax.all_to_all(
        term.reshape(replicas, shard, model), "dp", split_axis=0, concat_axis=0, tiled=True
    )
    saved = saved_hidden[0].transpose(0, 2, 1, 3)
    hidden_grad, scores = grads_of(rows, weight, saved, slot_prob, order, to_source)
    scores = lax.all_gather(scores.reshape(-1, 128), "expert", axis=0, tiled=True)
    scores = scores.reshape(groups * exp_dev, slots)
    returned = lax.dynamic_slice_in_dim(scores, me * capacity, capacity, axis=1)
    put = own_slot[:, None, :] == jnp.arange(capacity, dtype=jnp.int32)[None, :, None]
    by_token = jnp.sum(jnp.where(put, returned[..., None], 0.0), axis=1)
    prob_grad = jnp.sum(jnp.where(chose[:, 0], by_token[:, None, :], 0.0), axis=0).T
    down_grad = total_of(terms)
    return hidden_grad.transpose(0, 2, 1, 3)[None], prob_grad, down_grad[None]


def solution(mesh):
    tokens = P(("dp", "expert"), None)
    slots = P("dp", "expert", None, None, None)
    weights = P("expert", "dp", None)
    return jax.shard_map(
        on_device,
        mesh=mesh,
        in_specs=(tokens, tokens, tokens, slots, weights, P("expert")),
        out_specs=(slots, tokens, weights),
        check_vma=False,
    )
```

```python
import jax
import jax.numpy as jnp
from jax import lax
from jax.experimental import pallas as pl
from jax.experimental.pallas import tpu as pltpu
from jax.sharding import PartitionSpec as P

PACK = 4
SPAN = 1024


def pack_kernel(trained, tokens, token_of, weights, saved_t, *others):
    rows, term = others[-2:]
    experts, slots, _ = token_of.shape
    packs = tokens.shape[0] // (PACK * 128)
    part = slots // packs
    width = PACK * 128
    lanes = lax.broadcasted_iota(jnp.int32, (experts * part, width), 1)
    blocks = []
    for q in range(packs):
        wanted = jnp.concatenate(
            [token_of[j, q * part:(q + 1) * part] for j in range(experts)], axis=0
        )
        blocks.append(jnp.dot(
            (lanes == wanted).astype(jnp.bfloat16),
            tokens[q * width:(q + 1) * width],
            preferred_element_type=jnp.float32,
        ))
    packed = [
        jnp.concatenate([b[j * part:(j + 1) * part] for b in blocks], axis=0) for j in range(experts)
    ]
    for j in range(experts):
        rows[j] = packed[j].astype(jnp.bfloat16)
    chosen = jnp.where(trained[1] > 0, packed[1], packed[0])
    scaled = (weights[...] * chosen).astype(jnp.bfloat16)
    term[...] = jnp.dot(
        saved_t[...], scaled, preferred_element_type=jnp.float32
    ).astype(jnp.bfloat16)


def pack(tokens, token_of, weights, saved_t, trained, *later):
    count, model = tokens.shape
    experts, slots, _ = token_of.shape
    hidden = saved_t.shape[0]
    return pl.pallas_call(
        pack_kernel,
        grid=(model // SPAN,),
        in_specs=[
            pl.BlockSpec(memory_space=pltpu.SMEM),
            pl.BlockSpec((count, SPAN), lambda n: (0, n)),
            pl.BlockSpec((experts, slots, 1), lambda n: (0, 0, 0)),
            pl.BlockSpec((slots, 1), lambda n: (0, 0)),
            pl.BlockSpec((hidden, slots), lambda n: (0, 0)),
            *[pl.BlockSpec(memory_space=pl.ANY) for _ in later],
        ],
        out_specs=[
            pl.BlockSpec((experts, slots, SPAN), lambda n: (0, 0, n)),
            pl.BlockSpec((hidden, SPAN), lambda n: (0, n)),
        ],
        out_shape=[
            pltpu.HBM((experts, slots, model), jnp.bfloat16),
            pltpu.HBM((hidden, model), jnp.bfloat16),
        ],
        compiler_params=pltpu.CompilerParams(vmem_limit_bytes=48 << 20),
        cost_estimate=pl.CostEstimate(
            flops=2 * experts * slots * PACK * 128 * model + 2 * hidden * slots * model,
            bytes_accessed=2 * (count + experts * slots + hidden) * model,
            transcendentals=0,
        ),
    )(trained, tokens, token_of, weights, saved_t, *later)


def grad_kernel(rows, weight, saved, probs, order, to_source, hidden, scores):
    grads = lax.dot_general(
        rows[0],
        weight[:, 0].reshape(-1, weight.shape[-1]),
        (((1,), (1,)), ((), ())),
        preferred_element_type=jnp.float32,
    )
    width = grads.shape[1]
    saved_now = jnp.dot(
        to_source[...], saved[0].reshape(-1, width), preferred_element_type=jnp.float32
    )
    scores[0] = jnp.sum(grads * saved_now, axis=1, keepdims=True)
    scaled = (probs[0] * grads).astype(jnp.bfloat16)
    hidden[0] = jnp.dot(
        order[...], scaled, preferred_element_type=jnp.float32
    ).astype(jnp.bfloat16).reshape(hidden.shape[1:])


def half_orders(groups, capacity):
    some = groups // 2
    index = jnp.arange(some * capacity, dtype=jnp.int32)
    place = index % capacity * some + index // capacity
    order = place[None, :] == index[:, None]
    return order.astype(jnp.bfloat16), order.T.astype(jnp.bfloat16)


def grads_of(rows, weight, saved, probs, order, to_source):
    experts, slots, model = rows.shape
    _, capacity, groups, hidden = saved.shape
    halves = 2
    part, some = slots // halves, groups // halves
    shards, _, shard, _ = weight.shape
    return pl.pallas_call(
        grad_kernel,
        grid=(experts, halves),
        in_specs=[
            pl.BlockSpec((1, part, model), lambda j, i: (j, i, 0)),
            pl.BlockSpec((shards, 1, shard, model), lambda j, i: (0, j, 0, 0)),
            pl.BlockSpec((1, capacity, some, hidden), lambda j, i: (j, 0, i, 0)),
            pl.BlockSpec((1, part, 1), lambda j, i: (j, i, 0)),
            pl.BlockSpec((part, part), lambda j, i: (0, 0)),
            pl.BlockSpec((part, part), lambda j, i: (0, 0)),
        ],
        out_specs=[
            pl.BlockSpec((1, capacity, some, hidden), lambda j, i: (j, 0, i, 0)),
            pl.BlockSpec((1, part, 1), lambda j, i: (j, i, 0)),
        ],
        out_shape=[
            jax.ShapeDtypeStruct(saved.shape, jnp.bfloat16),
            jax.ShapeDtypeStruct((experts, slots, 1), jnp.float32),
        ],
        compiler_params=pltpu.CompilerParams(vmem_limit_bytes=48 << 20),
        cost_estimate=pl.CostEstimate(
            flops=2 * experts * slots * hidden * (model + 2 * part),
            bytes_accessed=2 * experts * (slots + hidden) * model + 4 * experts * slots * hidden,
            transcendentals=0,
        ),
    )(rows, weight, saved, probs, order, to_source)


def total_kernel(terms, total):
    replicas, shard, model = terms.shape
    span = 512
    for n in range(model // span):
        cut = slice(n * span, (n + 1) * span)
        total[:, cut] = jnp.sum(terms[:, :, cut].astype(jnp.float32), axis=0)


def total_of(terms):
    replicas, shard, model = terms.shape
    return pl.pallas_call(
        total_kernel,
        in_specs=[pl.BlockSpec(memory_space=pltpu.VMEM)],
        out_specs=pl.BlockSpec(memory_space=pltpu.VMEM),
        out_shape=jax.ShapeDtypeStruct((shard, model), jnp.float32),
        compiler_params=pltpu.CompilerParams(vmem_limit_bytes=16 << 20),
        cost_estimate=pl.CostEstimate(
            flops=replicas * shard * model,
            bytes_accessed=(2 * replicas + 4) * shard * model,
            transcendentals=0,
        ),
    )(pltpu.with_memory_space_constraint(terms, pltpu.VMEM))


def ranks_of(ids, experts):
    named = ids[None] == experts[:, None, None, None]
    taken = jnp.any(named, axis=2)
    place = jnp.arange(ids.shape[-1], dtype=jnp.int32)
    earlier = (place[:, None] < place[None, :]).astype(jnp.bfloat16)
    rank = lax.dot_general(
        taken.astype(jnp.bfloat16), earlier, (((2,), (0,)), ((), ())),
        preferred_element_type=jnp.float32,
    ).astype(jnp.int32)
    return named, taken, rank


def on_device(upstream, expert_ids, route_probs, saved_hidden, down_weight, trained):
    tok_rows, model = upstream.shape
    top = expert_ids.shape[1]
    groups = lax.axis_size("expert")
    replicas = lax.axis_size("dp")
    exp_dev, shard, _ = down_weight.shape
    capacity, hidden = saved_hidden.shape[3:]
    slots = groups * capacity

    tokens = lax.all_gather(upstream, "expert", axis=0, tiled=True)

    weight = lax.all_to_all(
        jnp.broadcast_to(down_weight[None], (replicas, exp_dev, shard, model)),
        "dp", split_axis=0, concat_axis=0, tiled=True,
    )

    routing = jnp.concatenate([expert_ids.T.astype(jnp.bfloat16), route_probs.T], axis=0)
    routing = lax.all_gather(routing, "expert", axis=0, tiled=True)
    routing = routing.reshape(groups, 2 * top, tok_rows)
    ids = routing[:, :top].astype(jnp.int32)
    probs = routing[:, top:].astype(jnp.float32)
    me = lax.axis_index("expert")
    own = me * exp_dev + jnp.arange(exp_dev, dtype=jnp.int32)
    named, taken, rank = ranks_of(ids, own)
    at_slot = taken[:, :, None, :] & (
        rank[:, :, None, :] == jnp.arange(capacity, dtype=jnp.int32)[None, None, :, None]
    )
    prob_of = jnp.sum(jnp.where(named, probs[None], 0.0), axis=2)
    place = jnp.arange(tok_rows, dtype=jnp.int32)
    local = (jnp.arange(groups, dtype=jnp.int32) % PACK)[:, None] * tok_rows + place[None, :]
    token_of = jnp.max(jnp.where(at_slot, local[None, :, None, :], -1), axis=3)
    slot_prob = jnp.sum(jnp.where(at_slot, prob_of[:, :, None, :], 0.0), axis=3)
    token_of = token_of.reshape(exp_dev, slots, 1)
    slot_prob = slot_prob.reshape(exp_dev, slots, 1)

    saved_t = jnp.where(trained[1] > 0, saved_hidden[0, 1], saved_hidden[0, 0])
    saved_t = saved_t.reshape(slots, hidden).T
    term_prob = jnp.where(trained[1] > 0, slot_prob[1], slot_prob[0])
    term_prob = jnp.where(jnp.max(trained) > 0, term_prob, 0.0)

    every = jnp.arange(groups * exp_dev, dtype=jnp.int32)
    chose, own_taken, own_rank = ranks_of(expert_ids.T[None], every)
    own_slot = jnp.where(own_taken, own_rank, -1)[:, 0]
    order, to_source = half_orders(groups, capacity)

    rows, term = pack(
        tokens, token_of, term_prob, saved_t, trained, slot_prob, order, to_source, own_slot
    )
    terms = lax.all_to_all(
        term.reshape(replicas, shard, model), "dp", split_axis=0, concat_axis=0, tiled=True
    )
    saved = saved_hidden[0].transpose(0, 2, 1, 3)
    hidden_grad, scores = grads_of(rows, weight, saved, slot_prob, order, to_source)
    scores = lax.all_gather(scores.reshape(-1, 128), "expert", axis=0, tiled=True)
    scores = scores.reshape(groups * exp_dev, slots)
    returned = lax.dynamic_slice_in_dim(scores, me * capacity, capacity, axis=1)
    put = own_slot[:, None, :] == jnp.arange(capacity, dtype=jnp.int32)[None, :, None]
    by_token = jnp.sum(jnp.where(put, returned[..., None], 0.0), axis=1)
    prob_grad = jnp.sum(jnp.where(chose[:, 0], by_token[:, None, :], 0.0), axis=0).T
    down_grad = total_of(terms)
    return hidden_grad.transpose(0, 2, 1, 3)[None], prob_grad, down_grad[None]


def solution(mesh):
    tokens = P(("dp", "expert"), None)
    slots = P("dp", "expert", None, None, None)
    weights = P("expert", "dp", None)
    return jax.shard_map(
        on_device,
        mesh=mesh,
        in_specs=(tokens, tokens, tokens, slots, weights, P("expert")),
        out_specs=(slots, tokens, weights),
        check_vma=False,
    )
```

```python
import jax
import jax.numpy as jnp
from jax import lax
from jax.experimental import pallas as pl
from jax.experimental.pallas import tpu as pltpu
from jax.sharding import PartitionSpec as P

PACK = 4
SPAN = 1024


def pack_kernel(trained, tokens, token_of, weights, saved_t, *others):
    rows, term = others[-2:]
    experts, slots, _ = token_of.shape
    packs = tokens.shape[0] // (PACK * 128)
    part = slots // packs
    width = PACK * 128
    lanes = lax.broadcasted_iota(jnp.int32, (experts * part, width), 1)
    blocks = []
    for q in range(packs):
        wanted = jnp.concatenate(
            [token_of[j, q * part:(q + 1) * part] for j in range(experts)], axis=0
        )
        blocks.append(jnp.dot(
            (lanes == wanted).astype(jnp.bfloat16),
            tokens[q * width:(q + 1) * width],
            preferred_element_type=jnp.float32,
        ))
    packed = [
        jnp.concatenate([b[j * part:(j + 1) * part] for b in blocks], axis=0) for j in range(experts)
    ]
    for j in range(experts):
        rows[j] = packed[j].astype(jnp.bfloat16)
    chosen = jnp.where(trained[1] > 0, packed[1], packed[0])
    scaled = (weights[...] * chosen).astype(jnp.bfloat16)
    term[...] = jnp.dot(
        saved_t[...], scaled, preferred_element_type=jnp.float32
    ).astype(jnp.bfloat16)


def pack(tokens, token_of, weights, saved_t, trained, *later):
    count, model = tokens.shape
    experts, slots, _ = token_of.shape
    hidden = saved_t.shape[0]
    return pl.pallas_call(
        pack_kernel,
        grid=(model // SPAN,),
        in_specs=[
            pl.BlockSpec(memory_space=pltpu.SMEM),
            pl.BlockSpec((count, SPAN), lambda n: (0, n)),
            pl.BlockSpec((experts, slots, 1), lambda n: (0, 0, 0)),
            pl.BlockSpec((slots, 1), lambda n: (0, 0)),
            pl.BlockSpec((hidden, slots), lambda n: (0, 0)),
            *[pl.BlockSpec(memory_space=pl.ANY) for _ in later],
        ],
        out_specs=[
            pl.BlockSpec((experts, slots, SPAN), lambda n: (0, 0, n)),
            pl.BlockSpec((hidden, SPAN), lambda n: (0, n)),
        ],
        out_shape=[
            pltpu.HBM((experts, slots, model), jnp.bfloat16),
            pltpu.HBM((hidden, model), jnp.bfloat16),
        ],
        compiler_params=pltpu.CompilerParams(vmem_limit_bytes=60 << 20),
        cost_estimate=pl.CostEstimate(
            flops=2 * experts * slots * PACK * 128 * model + 2 * hidden * slots * model,
            bytes_accessed=2 * (count + experts * slots + hidden) * model,
            transcendentals=0,
        ),
    )(trained, tokens, token_of, weights, saved_t, *later)


def grad_kernel(rows, weight, saved, probs, order, to_source, hidden, scores):
    grads = lax.dot_general(
        rows[0],
        weight[:, 0].reshape(-1, weight.shape[-1]),
        (((1,), (1,)), ((), ())),
        preferred_element_type=jnp.float32,
    )
    width = grads.shape[1]
    saved_now = jnp.dot(
        to_source[...], saved[0].reshape(-1, width), preferred_element_type=jnp.float32
    )
    scores[0] = jnp.sum(grads * saved_now, axis=1, keepdims=True)
    scaled = (probs[0] * grads).astype(jnp.bfloat16)
    hidden[0] = jnp.dot(
        order[...], scaled, preferred_element_type=jnp.float32
    ).astype(jnp.bfloat16).reshape(hidden.shape[1:])


def half_orders(groups, capacity):
    some = groups // 2
    index = jnp.arange(some * capacity, dtype=jnp.int32)
    place = index % capacity * some + index // capacity
    order = place[None, :] == index[:, None]
    return order.astype(jnp.bfloat16), order.T.astype(jnp.bfloat16)


def grads_of(rows, weight, saved, probs, order, to_source):
    experts, slots, model = rows.shape
    _, capacity, groups, hidden = saved.shape
    halves = 2
    part, some = slots // halves, groups // halves
    shards, _, shard, _ = weight.shape
    return pl.pallas_call(
        grad_kernel,
        grid=(experts, halves),
        in_specs=[
            pl.BlockSpec((1, part, model), lambda j, i: (j, i, 0)),
            pl.BlockSpec((shards, 1, shard, model), lambda j, i: (0, j, 0, 0)),
            pl.BlockSpec((1, capacity, some, hidden), lambda j, i: (j, 0, i, 0)),
            pl.BlockSpec((1, part, 1), lambda j, i: (j, i, 0)),
            pl.BlockSpec((part, part), lambda j, i: (0, 0)),
            pl.BlockSpec((part, part), lambda j, i: (0, 0)),
        ],
        out_specs=[
            pl.BlockSpec((1, capacity, some, hidden), lambda j, i: (j, 0, i, 0)),
            pl.BlockSpec((1, part, 1), lambda j, i: (j, i, 0)),
        ],
        out_shape=[
            jax.ShapeDtypeStruct(saved.shape, jnp.bfloat16),
            jax.ShapeDtypeStruct((experts, slots, 1), jnp.float32),
        ],
        compiler_params=pltpu.CompilerParams(vmem_limit_bytes=60 << 20),
        cost_estimate=pl.CostEstimate(
            flops=2 * experts * slots * hidden * (model + 2 * part),
            bytes_accessed=2 * experts * (slots + hidden) * model + 4 * experts * slots * hidden,
            transcendentals=0,
        ),
    )(rows, weight, saved, probs, order, to_source)


def total_kernel(terms, total):
    replicas, shard, model = terms.shape
    span = 512
    for n in range(model // span):
        cut = slice(n * span, (n + 1) * span)
        total[:, cut] = jnp.sum(terms[:, :, cut].astype(jnp.float32), axis=0)


def total_of(terms):
    replicas, shard, model = terms.shape
    return pl.pallas_call(
        total_kernel,
        in_specs=[pl.BlockSpec(memory_space=pltpu.VMEM)],
        out_specs=pl.BlockSpec(memory_space=pltpu.VMEM),
        out_shape=jax.ShapeDtypeStruct((shard, model), jnp.float32),
        compiler_params=pltpu.CompilerParams(vmem_limit_bytes=16 << 20),
        cost_estimate=pl.CostEstimate(
            flops=replicas * shard * model,
            bytes_accessed=(2 * replicas + 4) * shard * model,
            transcendentals=0,
        ),
    )(pltpu.with_memory_space_constraint(terms, pltpu.VMEM))


def ranks_of(ids, experts):
    named = ids[None] == experts[:, None, None, None]
    taken = jnp.any(named, axis=2)
    place = jnp.arange(ids.shape[-1], dtype=jnp.int32)
    earlier = (place[:, None] < place[None, :]).astype(jnp.bfloat16)
    rank = lax.dot_general(
        taken.astype(jnp.bfloat16), earlier, (((2,), (0,)), ((), ())),
        preferred_element_type=jnp.float32,
    ).astype(jnp.int32)
    return named, taken, rank


def on_device(upstream, expert_ids, route_probs, saved_hidden, down_weight, trained):
    tok_rows, model = upstream.shape
    top = expert_ids.shape[1]
    groups = lax.axis_size("expert")
    replicas = lax.axis_size("dp")
    exp_dev, shard, _ = down_weight.shape
    capacity, hidden = saved_hidden.shape[3:]
    slots = groups * capacity

    tokens = lax.all_gather(upstream, "expert", axis=0, tiled=True)

    weight = lax.all_to_all(
        jnp.broadcast_to(down_weight[None], (replicas, exp_dev, shard, model)),
        "dp", split_axis=0, concat_axis=0, tiled=True,
    )

    routing = jnp.concatenate([expert_ids.T.astype(jnp.bfloat16), route_probs.T], axis=0)
    routing = lax.all_gather(routing, "expert", axis=0, tiled=True)
    routing = routing.reshape(groups, 2 * top, tok_rows)
    ids = routing[:, :top].astype(jnp.int32)
    probs = routing[:, top:].astype(jnp.float32)
    me = lax.axis_index("expert")
    own = me * exp_dev + jnp.arange(exp_dev, dtype=jnp.int32)
    named, taken, rank = ranks_of(ids, own)
    at_slot = taken[:, :, None, :] & (
        rank[:, :, None, :] == jnp.arange(capacity, dtype=jnp.int32)[None, None, :, None]
    )
    prob_of = jnp.sum(jnp.where(named, probs[None], 0.0), axis=2)
    place = jnp.arange(tok_rows, dtype=jnp.int32)
    local = (jnp.arange(groups, dtype=jnp.int32) % PACK)[:, None] * tok_rows + place[None, :]
    token_of = jnp.max(jnp.where(at_slot, local[None, :, None, :], -1), axis=3)
    slot_prob = jnp.sum(jnp.where(at_slot, prob_of[:, :, None, :], 0.0), axis=3)
    token_of = token_of.reshape(exp_dev, slots, 1)
    slot_prob = slot_prob.reshape(exp_dev, slots, 1)

    saved_t = jnp.where(trained[1] > 0, saved_hidden[0, 1], saved_hidden[0, 0])
    saved_t = saved_t.reshape(slots, hidden).T
    term_prob = jnp.where(trained[1] > 0, slot_prob[1], slot_prob[0])
    term_prob = jnp.where(jnp.max(trained) > 0, term_prob, 0.0)

    every = jnp.arange(groups * exp_dev, dtype=jnp.int32)
    chose, own_taken, own_rank = ranks_of(expert_ids.T[None], every)
    own_slot = jnp.where(own_taken, own_rank, -1)[:, 0]
    order, to_source = half_orders(groups, capacity)

    rows, term = pack(
        tokens, token_of, term_prob, saved_t, trained, slot_prob, order, to_source, own_slot
    )
    terms = lax.all_to_all(
        term.reshape(replicas, shard, model), "dp", split_axis=0, concat_axis=0, tiled=True
    )
    saved = saved_hidden[0].transpose(0, 2, 1, 3)
    hidden_grad, scores = grads_of(rows, weight, saved, slot_prob, order, to_source)
    scores = lax.all_gather(scores.reshape(-1, 128), "expert", axis=0, tiled=True)
    scores = scores.reshape(groups * exp_dev, slots)
    returned = lax.dynamic_slice_in_dim(scores, me * capacity, capacity, axis=1)
    put = own_slot[:, None, :] == jnp.arange(capacity, dtype=jnp.int32)[None, :, None]
    by_token = jnp.sum(jnp.where(put, returned[..., None], 0.0), axis=1)
    prob_grad = jnp.sum(jnp.where(chose[:, 0], by_token[:, None, :], 0.0), axis=0).T
    down_grad = total_of(terms)
    return hidden_grad.transpose(0, 2, 1, 3)[None], prob_grad, down_grad[None]


def solution(mesh):
    tokens = P(("dp", "expert"), None)
    slots = P("dp", "expert", None, None, None)
    weights = P("expert", "dp", None)
    return jax.shard_map(
        on_device,
        mesh=mesh,
        in_specs=(tokens, tokens, tokens, slots, weights, P("expert")),
        out_specs=(slots, tokens, weights),
        check_vma=False,
    )
```

```python
import jax
import jax.numpy as jnp
from jax import lax
from jax.experimental import pallas as pl
from jax.experimental.pallas import tpu as pltpu
from jax.sharding import PartitionSpec as P

PACK = 4
SPAN = 1024


def pack_kernel(trained, tokens, token_of, weights, saved_t, *others):
    rows, term = others[-2:]
    experts, slots, _ = token_of.shape
    packs = tokens.shape[0] // (PACK * 128)
    part = slots // packs
    width = PACK * 128
    lanes = lax.broadcasted_iota(jnp.int32, (experts * part, width), 1)
    blocks = []
    for q in range(packs):
        wanted = jnp.concatenate(
            [token_of[j, q * part:(q + 1) * part] for j in range(experts)], axis=0
        )
        blocks.append(jnp.dot(
            (lanes == wanted).astype(jnp.bfloat16),
            tokens[q * width:(q + 1) * width],
            preferred_element_type=jnp.float32,
        ))
    packed = [
        jnp.concatenate([b[j * part:(j + 1) * part] for b in blocks], axis=0) for j in range(experts)
    ]
    for j in range(experts):
        rows[j] = packed[j].astype(jnp.bfloat16)
    chosen = jnp.where(trained[1] > 0, packed[1], packed[0])
    scaled = (weights[...] * chosen).astype(jnp.bfloat16)
    term[...] = jnp.dot(
        saved_t[...], scaled, preferred_element_type=jnp.float32
    ).astype(jnp.bfloat16)


def pack(tokens, token_of, weights, saved_t, trained, *later):
    count, model = tokens.shape
    experts, slots, _ = token_of.shape
    hidden = saved_t.shape[0]
    return pl.pallas_call(
        pack_kernel,
        grid=(model // SPAN,),
        in_specs=[
            pl.BlockSpec(memory_space=pltpu.SMEM),
            pl.BlockSpec((count, SPAN), lambda n: (0, n)),
            pl.BlockSpec((experts, slots, 1), lambda n: (0, 0, 0)),
            pl.BlockSpec((slots, 1), lambda n: (0, 0)),
            pl.BlockSpec((hidden, slots), lambda n: (0, 0)),
            *[pl.BlockSpec(memory_space=pl.ANY) for _ in later],
        ],
        out_specs=[
            pl.BlockSpec((experts, slots, SPAN), lambda n: (0, 0, n)),
            pl.BlockSpec((hidden, SPAN), lambda n: (0, n)),
        ],
        out_shape=[
            pltpu.HBM((experts, slots, model), jnp.bfloat16),
            pltpu.HBM((hidden, model), jnp.bfloat16),
        ],
        compiler_params=pltpu.CompilerParams(vmem_limit_bytes=60 << 20),
        cost_estimate=pl.CostEstimate(
            flops=2 * experts * slots * PACK * 128 * model + 2 * hidden * slots * model,
            bytes_accessed=2 * (count + experts * slots + hidden) * model,
            transcendentals=0,
        ),
    )(trained, tokens, token_of, weights, saved_t, *later)


def grad_kernel(rows, weight, saved, probs, order, to_source, hidden, scores):
    grads = lax.dot_general(
        rows[0],
        weight[:, 0].reshape(-1, weight.shape[-1]),
        (((1,), (1,)), ((), ())),
        preferred_element_type=jnp.float32,
    )
    width = grads.shape[1]
    saved_now = jnp.dot(
        to_source[...], saved[0].reshape(-1, width), preferred_element_type=jnp.float32
    )
    scores[0] = jnp.sum(grads * saved_now, axis=1, keepdims=True)
    scaled = (probs[0] * grads).astype(jnp.bfloat16)
    hidden[0] = jnp.dot(
        order[...], scaled, preferred_element_type=jnp.float32
    ).astype(jnp.bfloat16).reshape(hidden.shape[1:])


def half_orders(groups, capacity):
    some = groups // 2
    index = jnp.arange(some * capacity, dtype=jnp.int32)
    place = index % capacity * some + index // capacity
    order = place[None, :] == index[:, None]
    return order.astype(jnp.bfloat16), order.T.astype(jnp.bfloat16)


def grads_of(rows, weight, saved, probs, order, to_source):
    experts, slots, model = rows.shape
    _, capacity, groups, hidden = saved.shape
    halves = 2
    part, some = slots // halves, groups // halves
    shards, _, shard, _ = weight.shape
    return pl.pallas_call(
        grad_kernel,
        grid=(experts, halves),
        in_specs=[
            pl.BlockSpec((1, part, model), lambda j, i: (j, i, 0)),
            pl.BlockSpec((shards, 1, shard, model), lambda j, i: (0, j, 0, 0)),
            pl.BlockSpec((1, capacity, some, hidden), lambda j, i: (j, 0, i, 0)),
            pl.BlockSpec((1, part, 1), lambda j, i: (j, i, 0)),
            pl.BlockSpec((part, part), lambda j, i: (0, 0)),
            pl.BlockSpec((part, part), lambda j, i: (0, 0)),
        ],
        out_specs=[
            pl.BlockSpec((1, capacity, some, hidden), lambda j, i: (j, 0, i, 0)),
            pl.BlockSpec((1, part, 1), lambda j, i: (j, i, 0)),
        ],
        out_shape=[
            jax.ShapeDtypeStruct(saved.shape, jnp.bfloat16),
            jax.ShapeDtypeStruct((experts, slots, 1), jnp.float32),
        ],
        compiler_params=pltpu.CompilerParams(vmem_limit_bytes=60 << 20),
        cost_estimate=pl.CostEstimate(
            flops=2 * experts * slots * hidden * (model + 2 * part),
            bytes_accessed=2 * experts * (slots + hidden) * model + 4 * experts * slots * hidden,
            transcendentals=0,
        ),
    )(rows, weight, saved, probs, order, to_source)


def total_kernel(terms, total):
    replicas, shard, model = terms.shape
    span = 512
    for n in range(model // span):
        cut = slice(n * span, (n + 1) * span)
        total[:, cut] = jnp.sum(terms[:, :, cut].astype(jnp.float32), axis=0)


def total_of(terms):
    replicas, shard, model = terms.shape
    return pl.pallas_call(
        total_kernel,
        in_specs=[pl.BlockSpec(memory_space=pltpu.VMEM)],
        out_specs=pl.BlockSpec(memory_space=pltpu.VMEM),
        out_shape=jax.ShapeDtypeStruct((shard, model), jnp.float32),
        compiler_params=pltpu.CompilerParams(vmem_limit_bytes=16 << 20),
        cost_estimate=pl.CostEstimate(
            flops=replicas * shard * model,
            bytes_accessed=(2 * replicas + 4) * shard * model,
            transcendentals=0,
        ),
    )(pltpu.with_memory_space_constraint(terms, pltpu.VMEM))


def ranks_of(ids, experts):
    named = ids[None] == experts[:, None, None, None]
    taken = jnp.any(named, axis=2)
    place = jnp.arange(ids.shape[-1], dtype=jnp.int32)
    earlier = (place[:, None] < place[None, :]).astype(jnp.bfloat16)
    rank = lax.dot_general(
        taken.astype(jnp.bfloat16), earlier, (((2,), (0,)), ((), ())),
        preferred_element_type=jnp.float32,
    ).astype(jnp.int32)
    return named, taken, rank


def on_device(upstream, expert_ids, route_probs, saved_hidden, down_weight, trained):
    tok_rows, model = upstream.shape
    top = expert_ids.shape[1]
    groups = lax.axis_size("expert")
    replicas = lax.axis_size("dp")
    exp_dev, shard, _ = down_weight.shape
    capacity, hidden = saved_hidden.shape[3:]
    slots = groups * capacity

    tokens = lax.all_gather(upstream, "expert", axis=0, tiled=True)

    weight = lax.all_to_all(
        jnp.broadcast_to(down_weight[None], (replicas, exp_dev, shard, model)),
        "dp", split_axis=0, concat_axis=0, tiled=True,
    )

    routing = jnp.concatenate([expert_ids.T.astype(jnp.bfloat16), route_probs.T], axis=0)
    routing = lax.all_gather(routing, "expert", axis=0, tiled=True)
    routing = routing.reshape(groups, 2 * top, tok_rows)
    ids = routing[:, :top].astype(jnp.int32)
    probs = routing[:, top:].astype(jnp.float32)
    me = lax.axis_index("expert")
    own = me * exp_dev + jnp.arange(exp_dev, dtype=jnp.int32)
    named, taken, rank = ranks_of(ids, own)
    at_slot = taken[:, :, None, :] & (
        rank[:, :, None, :] == jnp.arange(capacity, dtype=jnp.int32)[None, None, :, None]
    )
    prob_of = jnp.sum(jnp.where(named, probs[None], 0.0), axis=2)
    place = jnp.arange(tok_rows, dtype=jnp.int32)
    local = (jnp.arange(groups, dtype=jnp.int32) % PACK)[:, None] * tok_rows + place[None, :]
    token_of = jnp.max(jnp.where(at_slot, local[None, :, None, :], -1), axis=3)
    slot_prob = jnp.sum(jnp.where(at_slot, prob_of[:, :, None, :], 0.0), axis=3)
    token_of = token_of.reshape(exp_dev, slots, 1)
    slot_prob = slot_prob.reshape(exp_dev, slots, 1)

    saved_t = jnp.where(trained[1] > 0, saved_hidden[0, 1], saved_hidden[0, 0])
    saved_t = saved_t.reshape(slots, hidden).T
    term_prob = jnp.where(trained[1] > 0, slot_prob[1], slot_prob[0])
    term_prob = jnp.where(jnp.max(trained) > 0, term_prob, 0.0)

    every = jnp.arange(groups * exp_dev, dtype=jnp.int32)
    chose, own_taken, own_rank = ranks_of(expert_ids.T[None], every)
    own_slot = jnp.where(own_taken, own_rank, -1)[:, 0]
    order, to_source = half_orders(groups, capacity)

    rows, term = pack(
        tokens, token_of, term_prob, saved_t, trained, slot_prob, order, to_source, own_slot
    )
    terms = lax.all_to_all(
        term.reshape(replicas, shard, model), "dp", split_axis=0, concat_axis=0, tiled=True
    )
    saved = saved_hidden[0].transpose(0, 2, 1, 3)
    hidden_grad, scores = grads_of(rows, weight, saved, slot_prob, order, to_source)
    scores = lax.all_gather(scores.reshape(exp_dev, slots), "expert", axis=0, tiled=True)
    returned = lax.dynamic_slice_in_dim(scores, me * capacity, capacity, axis=1)
    put = own_slot[:, None, :] == jnp.arange(capacity, dtype=jnp.int32)[None, :, None]
    by_token = jnp.sum(jnp.where(put, returned[..., None], 0.0), axis=1)
    prob_grad = jnp.sum(jnp.where(chose[:, 0], by_token[:, None, :], 0.0), axis=0).T
    down_grad = total_of(terms)
    return hidden_grad.transpose(0, 2, 1, 3)[None], prob_grad, down_grad[None]


def solution(mesh):
    tokens = P(("dp", "expert"), None)
    slots = P("dp", "expert", None, None, None)
    weights = P("expert", "dp", None)
    return jax.shard_map(
        on_device,
        mesh=mesh,
        in_specs=(tokens, tokens, tokens, slots, weights, P("expert")),
        out_specs=(slots, tokens, weights),
        check_vma=False,
    )
```

```python
import jax
import jax.numpy as jnp
from jax import lax
from jax.experimental import pallas as pl
from jax.experimental.pallas import tpu as pltpu
from jax.sharding import PartitionSpec as P

PACK = 4
SPAN = 1024


def pack_kernel(trained, tokens, token_of, weights, saved_t, *others):
    rows, term = others[-2:]
    experts, slots, _ = token_of.shape
    packs = tokens.shape[0] // (PACK * 128)
    part = slots // packs
    width = PACK * 128
    lanes = lax.broadcasted_iota(jnp.int32, (experts * part, width), 1)
    blocks = []
    for q in range(packs):
        wanted = jnp.concatenate(
            [token_of[j, q * part:(q + 1) * part] for j in range(experts)], axis=0
        )
        blocks.append(jnp.dot(
            (lanes == wanted).astype(jnp.bfloat16),
            tokens[q * width:(q + 1) * width],
            preferred_element_type=jnp.float32,
        ))
    packed = [
        jnp.concatenate([b[j * part:(j + 1) * part] for b in blocks], axis=0) for j in range(experts)
    ]
    for j in range(experts):
        rows[j] = packed[j].astype(jnp.bfloat16)
    chosen = jnp.where(trained[1] > 0, packed[1], packed[0])
    scaled = (weights[...] * chosen).astype(jnp.bfloat16)
    term[...] = jnp.dot(
        saved_t[...], scaled, preferred_element_type=jnp.float32
    ).astype(jnp.bfloat16)


def pack(tokens, token_of, weights, saved_t, trained, *later):
    count, model = tokens.shape
    experts, slots, _ = token_of.shape
    hidden = saved_t.shape[0]
    return pl.pallas_call(
        pack_kernel,
        grid=(model // SPAN,),
        in_specs=[
            pl.BlockSpec(memory_space=pltpu.SMEM),
            pl.BlockSpec((count, SPAN), lambda n: (0, n)),
            pl.BlockSpec((experts, slots, 1), lambda n: (0, 0, 0)),
            pl.BlockSpec((slots, 1), lambda n: (0, 0)),
            pl.BlockSpec((hidden, slots), lambda n: (0, 0)),
            *[pl.BlockSpec(memory_space=pl.ANY) for _ in later],
        ],
        out_specs=[
            pl.BlockSpec((experts, slots, SPAN), lambda n: (0, 0, n)),
            pl.BlockSpec((hidden, SPAN), lambda n: (0, n)),
        ],
        out_shape=[
            pltpu.HBM((experts, slots, model), jnp.bfloat16),
            pltpu.HBM((hidden, model), jnp.bfloat16),
        ],
        compiler_params=pltpu.CompilerParams(vmem_limit_bytes=48 << 20),
        cost_estimate=pl.CostEstimate(
            flops=2 * experts * slots * PACK * 128 * model + 2 * hidden * slots * model,
            bytes_accessed=2 * (count + experts * slots + hidden) * model,
            transcendentals=0,
        ),
    )(trained, tokens, token_of, weights, saved_t, *later)


def grad_kernel(rows, weight, saved, probs, order, to_source, hidden, scores):
    grads = lax.dot_general(
        rows[0],
        weight[:, 0].reshape(-1, weight.shape[-1]),
        (((1,), (1,)), ((), ())),
        preferred_element_type=jnp.float32,
    )
    width = grads.shape[1]
    saved_now = jnp.dot(
        to_source[...], saved[0].reshape(-1, width), preferred_element_type=jnp.float32
    )
    scores[0] = jnp.sum(grads * saved_now, axis=1, keepdims=True)
    scaled = (probs[0] * grads).astype(jnp.bfloat16)
    hidden[0] = jnp.dot(
        order[...], scaled, preferred_element_type=jnp.float32
    ).astype(jnp.bfloat16).reshape(hidden.shape[1:])


def half_orders(groups, capacity):
    some = groups // 2
    index = jnp.arange(some * capacity, dtype=jnp.int32)
    place = index % capacity * some + index // capacity
    order = place[None, :] == index[:, None]
    return order.astype(jnp.bfloat16), order.T.astype(jnp.bfloat16)


def grads_of(rows, weight, saved, probs, order, to_source):
    experts, slots, model = rows.shape
    _, capacity, groups, hidden = saved.shape
    halves = 2
    part, some = slots // halves, groups // halves
    shards, _, shard, _ = weight.shape
    return pl.pallas_call(
        grad_kernel,
        grid=(experts, halves),
        in_specs=[
            pl.BlockSpec((1, part, model), lambda j, i: (j, i, 0)),
            pl.BlockSpec((shards, 1, shard, model), lambda j, i: (0, j, 0, 0)),
            pl.BlockSpec((1, capacity, some, hidden), lambda j, i: (j, 0, i, 0)),
            pl.BlockSpec((1, part, 1), lambda j, i: (j, i, 0)),
            pl.BlockSpec((part, part), lambda j, i: (0, 0)),
            pl.BlockSpec((part, part), lambda j, i: (0, 0)),
        ],
        out_specs=[
            pl.BlockSpec((1, capacity, some, hidden), lambda j, i: (j, 0, i, 0)),
            pl.BlockSpec((1, part, 1), lambda j, i: (j, i, 0)),
        ],
        out_shape=[
            jax.ShapeDtypeStruct(saved.shape, jnp.bfloat16),
            jax.ShapeDtypeStruct((experts, slots, 1), jnp.float32),
        ],
        compiler_params=pltpu.CompilerParams(vmem_limit_bytes=48 << 20),
        cost_estimate=pl.CostEstimate(
            flops=2 * experts * slots * hidden * (model + 2 * part),
            bytes_accessed=2 * experts * (slots + hidden) * model + 4 * experts * slots * hidden,
            transcendentals=0,
        ),
    )(rows, weight, saved, probs, order, to_source)


def total_kernel(*refs):
    *terms, total = refs
    total[...] = sum(jnp.sum(t[...].astype(jnp.float32), axis=0) for t in terms)


def total_of(terms):
    replicas, shard, model = terms.shape
    span, cuts = model // 2, min(4, replicas)
    return pl.pallas_call(
        total_kernel,
        grid=(model // span,),
        in_specs=[
            pl.BlockSpec((replicas // cuts, shard, span), lambda n, q=q: (q, 0, n))
            for q in range(cuts)
        ],
        out_specs=pl.BlockSpec((shard, span), lambda n: (0, n)),
        out_shape=jax.ShapeDtypeStruct((shard, model), jnp.float32),
        cost_estimate=pl.CostEstimate(
            flops=replicas * shard * model,
            bytes_accessed=(2 * replicas + 4) * shard * model,
            transcendentals=0,
        ),
    )(*[terms] * cuts)


def ranks_of(ids, experts):
    named = ids[None] == experts[:, None, None, None]
    taken = jnp.any(named, axis=2)
    place = jnp.arange(ids.shape[-1], dtype=jnp.int32)
    earlier = (place[:, None] < place[None, :]).astype(jnp.bfloat16)
    rank = lax.dot_general(
        taken.astype(jnp.bfloat16), earlier, (((2,), (0,)), ((), ())),
        preferred_element_type=jnp.float32,
    ).astype(jnp.int32)
    return named, taken, rank


def on_device(upstream, expert_ids, route_probs, saved_hidden, down_weight, trained):
    tok_rows, model = upstream.shape
    top = expert_ids.shape[1]
    groups = lax.axis_size("expert")
    replicas = lax.axis_size("dp")
    exp_dev, shard, _ = down_weight.shape
    capacity, hidden = saved_hidden.shape[3:]
    slots = groups * capacity

    tokens = lax.all_gather(upstream, "expert", axis=0, tiled=True)

    weight = lax.all_to_all(
        jnp.broadcast_to(down_weight[None], (replicas, exp_dev, shard, model)),
        "dp", split_axis=0, concat_axis=0, tiled=True,
    )

    routing = jnp.concatenate([expert_ids.T.astype(jnp.bfloat16), route_probs.T], axis=0)
    routing = lax.all_gather(routing, "expert", axis=0, tiled=True)
    routing = routing.reshape(groups, 2 * top, tok_rows)
    ids = routing[:, :top].astype(jnp.int32)
    probs = routing[:, top:].astype(jnp.float32)
    me = lax.axis_index("expert")
    own = me * exp_dev + jnp.arange(exp_dev, dtype=jnp.int32)
    named, taken, rank = ranks_of(ids, own)
    at_slot = taken[:, :, None, :] & (
        rank[:, :, None, :] == jnp.arange(capacity, dtype=jnp.int32)[None, None, :, None]
    )
    prob_of = jnp.sum(jnp.where(named, probs[None], 0.0), axis=2)
    place = jnp.arange(tok_rows, dtype=jnp.int32)
    local = (jnp.arange(groups, dtype=jnp.int32) % PACK)[:, None] * tok_rows + place[None, :]
    token_of = jnp.max(jnp.where(at_slot, local[None, :, None, :], -1), axis=3)
    slot_prob = jnp.sum(jnp.where(at_slot, prob_of[:, :, None, :], 0.0), axis=3)
    token_of = token_of.reshape(exp_dev, slots, 1)
    slot_prob = slot_prob.reshape(exp_dev, slots, 1)

    saved_t = jnp.where(trained[1] > 0, saved_hidden[0, 1], saved_hidden[0, 0])
    saved_t = saved_t.reshape(slots, hidden).T
    term_prob = jnp.where(trained[1] > 0, slot_prob[1], slot_prob[0])
    term_prob = jnp.where(jnp.max(trained) > 0, term_prob, 0.0)

    every = jnp.arange(groups * exp_dev, dtype=jnp.int32)
    chose, own_taken, own_rank = ranks_of(expert_ids.T[None], every)
    own_slot = jnp.where(own_taken, own_rank, -1)[:, 0]
    order, to_source = half_orders(groups, capacity)

    rows, term = pack(
        tokens, token_of, term_prob, saved_t, trained, slot_prob, order, to_source, own_slot
    )
    terms = lax.all_to_all(
        term.reshape(replicas, shard, model), "dp", split_axis=0, concat_axis=0, tiled=True
    )
    saved = saved_hidden[0].transpose(0, 2, 1, 3)
    hidden_grad, scores = grads_of(rows, weight, saved, slot_prob, order, to_source)
    scores = lax.all_gather(scores.reshape(exp_dev, slots), "expert", axis=0, tiled=True)
    returned = lax.dynamic_slice_in_dim(scores, me * capacity, capacity, axis=1)
    put = own_slot[:, None, :] == jnp.arange(capacity, dtype=jnp.int32)[None, :, None]
    by_token = jnp.sum(jnp.where(put, returned[..., None], 0.0), axis=1)
    prob_grad = jnp.sum(jnp.where(chose[:, 0], by_token[:, None, :], 0.0), axis=0).T
    down_grad = total_of(terms)
    return hidden_grad.transpose(0, 2, 1, 3)[None], prob_grad, down_grad[None]


def solution(mesh):
    tokens = P(("dp", "expert"), None)
    slots = P("dp", "expert", None, None, None)
    weights = P("expert", "dp", None)
    return jax.shard_map(
        on_device,
        mesh=mesh,
        in_specs=(tokens, tokens, tokens, slots, weights, P("expert")),
        out_specs=(slots, tokens, weights),
        check_vma=False,
    )
```
